256 devices in a mesh: dp: 8 (over x, y_hi), expert: 32 (over y_lo, z, core).
Axes of the slice: x: 4, y: 4 (y_hi: 2, y_lo: 2; y = y_hi * 2 + y_lo), z: 8, core: 2. Of those that a mesh axis runs over, the one named last changes fastest.
Arguments:
- patches: bfloat16 [32768, 1280], P(('dp', 'expert')), may hold values from -6 to 6
- teacher: bfloat16 [32768, 1280], P(('dp', 'expert')), may hold values from -6 to 6
- route: int32 [32768, 1], P(('dp', 'expert')), may hold values from 0 to 31; in each aligned block of 128 rows (0 to 127, 128 to 255, ...) at most 8 rows name the same one
- gates: bfloat16 [32768], P(('dp', 'expert')), may hold values from 0.25 to 1
- w_in: bfloat16 [32, 40, 128, 128], P('expert'), may hold values from -0.5 to 0.5
- in_rows: int32 [32, 40], P('expert'), may hold values from 0 to 9
- in_cols: int32 [32, 40], P('expert'), may hold values from 0 to 39, each once within a row
- w_out: bfloat16 [32, 40, 128, 128], P('expert'), may hold values from -0.25 to 0.25
- out_rows: int32 [32, 40], P('expert'), may hold values from 0 to 39
Outputs:
- student: bfloat16 [32768, 1280], P(('dp', 'expert'))
- grad_patches: float32 [32768, 1280], P(('dp', 'expert'))
- grad_w_in: float32 [32, 40, 128, 128], P('expert', 'dp')
- grad_w_out: float32 [32, 40, 128, 128], P('expert', 'dp')
The draws below stay inside these ranges and needn't reach their ends.
Inputs may be any that keep to these rules, and one draw needn't show every extreme that they name: `route`: within the rows of one device no expert is named by more than 8 rows, a bound that some block reaches. in_rows[e, b] is the feature block read by block b of expert e's first matrix. Each row of in_cols names every hidden block once. Block m of expert e's second matrix reads hidden block out_rows[e, m] and writes output block m // 4.
All inputs are finite; a program needn't handle non-finite values.
Results may differ from the reference program's by a relative error of at most 0.014.
Values may be sent and summed in bfloat16 or wider, within the bound.
No kernel may reach another device: no remote copies, remote signals or barrier semaphores. Data moves between devices by JAX's collectives and lax.ppermute only.
A program may use at most 64 MiB of HBM per device.

```python
import math
import jax
import jax.numpy as jnp
import numpy as np
from jax import lax

D = 1280
EXPERTS = 32
BLK = 128
K2 = 4
TOK_DEV = 128
CAP = 8
TOKENS = 32768
ROWB = 256
DB = 10
FB = 40
NB2 = 40
N_DP = 8
N_EXPERT = 32


def plant(drawn, stream_key, smallest, largest):
    index_at = [jax.random.randint(jax.random.fold_in(stream_key, axis), (), 0, length) for axis, length in enumerate(drawn.shape)]
    widest = drawn.shape.index(max(drawn.shape))
    next_to = index_at[:widest] + [(index_at[widest] + 1) % drawn.shape[widest]] + index_at[widest + 1:]
    return drawn.at[tuple(index_at)].set(smallest).at[tuple(next_to)].set(largest)


def block_scale(stream_key, extent, split, low, top_value):
    factor_of, own = 1.0, jax.random.fold_in(stream_key, 6)
    for dim, shards_of in split:
        steps = jnp.exp(jax.random.uniform(jax.random.fold_in(own, dim), (shards_of,), jnp.float32, low / len(split), top_value / len(split)))
        factor_of = factor_of * jnp.repeat(steps, extent[dim] // shards_of).reshape([-1 if axis == dim else 1 for axis in range(len(extent))])
    return factor_of


def shared_out(key, own, number, rows, amount, top, most, skew):
    ranking = jax.random.permutation(key, amount)
    packed, usual = load_shares(amount, rows * top, most, skew, True), load_shares(amount, rows * top, most, skew, False)
    places = jnp.arange(amount)

    def named(sizes, offset_by):
        used = int((sizes > 0).sum())
        fixed = max(1, used // 4)
        moved = fixed + (places - fixed + offset_by * (used - fixed)) % max(1, amount - fixed)
        return jnp.zeros((amount,), jnp.int32).at[ranking[jnp.where(places < fixed, places, moved)]].set(jnp.asarray(sizes, jnp.int32))

    sizes = jnp.where(number % 4 == 0, named(packed, number // 4), named(usual, number - number // 4 - 1))
    mixed = jax.random.permutation(jax.random.fold_in(own, 3), amount)
    source_of, taker = mixed[0:amount // 2 * 2:2], mixed[1:amount // 2 * 2:2]
    room = jnp.minimum(sizes[source_of] - 1, most - sizes[taker]) // 2
    room = jnp.where((source_of == ranking[0]) | (taker == ranking[0]) | (sizes[taker] == 0), 0, jnp.maximum(room, 0))
    moved = jax.random.randint(jax.random.fold_in(own, 4), (amount // 2,), 0, 1 << 20) % (room + 1)
    sizes = sizes.at[source_of].add(-moved).at[taker].add(moved)
    items = jnp.searchsorted(jnp.cumsum(sizes), jnp.arange(rows * top), side="right").astype(jnp.int32)
    listing = items.reshape(top, rows).T
    listing = listing[jax.random.permutation(jax.random.fold_in(own, 1), rows)]
    offset_by = jax.random.randint(jax.random.fold_in(own, 2), (rows, 1), 0, top)
    return jnp.take_along_axis(listing, (jnp.arange(top)[None, :] + offset_by) % top, axis=1)


def load_shares(number_of, total, most, skew, full):
    portions = [(1 << 20) // math.isqrt(standing ** skew) + 1 for standing in range(1, number_of + 1)]
    largest = most if full else min(most, max(-(-total // number_of), total * portions[0] // sum(portions)))
    least = 1 if total - largest >= number_of - 1 else 0
    given, spare = [largest] + [least] * (number_of - 1), total - largest - least * (number_of - 1)
    while spare > 0:
        candidates = [i for i in range(1, number_of) if given[i] < largest] or [i for i in range(1, number_of) if given[i] < most]
        mass, budget = sum([portions[i] for i in candidates]), spare
        for i in candidates:
            more = min(most - given[i], max(1, budget * portions[i] // mass), spare)
            given[i] = given[i] + more
            spare = spare - more
    return np.array(given)


def normal_values(own_key, dims, scale, bound, cuts=(), held_as=jnp.bfloat16):
    loudness = block_scale(own_key, dims, cuts, -0.22, 0.18) if cuts else 1.0
    result = jax.random.normal(own_key, dims, jnp.float32) * scale * loudness
    return jnp.minimum(jnp.maximum(result, -bound), bound).astype(held_as)


def setup_inputs(seed: int = 0) -> dict:
    seeds = jax.random.split(jax.random.key(seed), 10)
    patches = normal_values(seeds[0], (TOKENS, D), 1.0, 6.0, ((0, 256),))
    teacher = normal_values(seeds[1], (TOKENS, D), 1.0, 6.0, ((0, 256),))
    route_keys = jax.random.split(jax.random.fold_in(seeds[2], 1), TOKENS // TOK_DEV)
    route_turns = jax.random.permutation(jax.random.fold_in(seeds[2], 3), TOKENS // TOK_DEV)
    route = jax.vmap(lambda own, number: shared_out(jax.random.fold_in(seeds[2], 2), own, number, TOK_DEV, EXPERTS, 1, CAP, 2))(route_keys, route_turns).reshape((TOKENS, 1))
    gates = jnp.clip(0.25 + 0.75 * jax.random.uniform(seeds[3], (TOKENS,), jnp.float32) ** block_scale(seeds[3], (TOKENS,), ((0, 256),), -0.2, 0.2), 0.25, 1.0).astype(jnp.bfloat16)
    w_in = normal_values(seeds[4], (EXPERTS, FB, BLK, BLK), BLK ** -0.5, 0.5, ((0, 32),))
    in_rows = plant(jax.random.randint(seeds[5], (EXPERTS, FB), 0, DB), jax.random.fold_in(seeds[5], 1), 0, DB - 1).astype(jnp.int32)
    in_cols = jax.vmap(lambda own: jax.random.permutation(own, FB))(jax.random.split(seeds[6], EXPERTS)).reshape((EXPERTS, FB)).astype(jnp.int32)
    w_out = normal_values(seeds[7], (EXPERTS, NB2, BLK, BLK), (K2 * BLK) ** -0.5, 0.25, ((0, 32),))
    out_rows = plant(jax.random.randint(seeds[8], (EXPERTS, NB2), 0, FB), jax.random.fold_in(seeds[8], 1), 0, FB - 1).astype(jnp.int32)
    return {"patches": patches, "teacher": teacher, "route": route, "gates": gates, "w_in": w_in, "in_rows": in_rows, "in_cols": in_cols, "w_out": w_out, "out_rows": out_rows}


def normalize(features):
    centred = features - lax.optimization_barrier(jnp.mean(features, axis=-1, keepdims=True))
    variance = lax.optimization_barrier(jnp.mean(centred * centred, axis=-1, keepdims=True))
    return centred * lax.rsqrt(variance + 1e-06)

def hidden_order(columns):
    labels = jnp.arange(FB, dtype=jnp.int32)
    matches = columns[:, None] == labels[None, :]
    return lax.optimization_barrier(jnp.sum(jnp.where(matches, labels[:, None], 0), axis=0)).astype(jnp.int32)

def expert_hidden(normed_rows, weight_in, rows_in, read_blocks):
    row_count = normed_rows.shape[0]
    picked = jnp.take(normed_rows.reshape(row_count, DB, BLK), rows_in, axis=1)
    pre_hidden = jnp.einsum('rbi,bio->rbo', picked.astype(jnp.float32), weight_in.astype(jnp.float32))
    hidden = jax.nn.gelu(pre_hidden).astype(jnp.bfloat16)
    spread = jnp.take(hidden, read_blocks, axis=1).reshape(row_count, DB, K2, BLK)
    return (picked, pre_hidden, spread)

def expert_output(spread, weight_out):
    out_blocks = weight_out.reshape(DB, K2, BLK, BLK)
    produced = jnp.einsum('rjkf,jkfd->rjd', spread.astype(jnp.float32), out_blocks.astype(jnp.float32))
    return produced.reshape(spread.shape[0], D)

def expert_backward(grad_out_rows, picked, pre_hidden, spread, weight_in, rows_in, weight_out, read_blocks):
    row_count = grad_out_rows.shape[0]
    grad_blocks = grad_out_rows.reshape(row_count, DB, BLK).astype(jnp.float32)
    out_blocks = weight_out.reshape(DB, K2, BLK, BLK).astype(jnp.float32)
    grad_weight_out = jnp.einsum('rjkf,rjd->jkfd', spread.astype(jnp.float32), grad_blocks).reshape(NB2, BLK, BLK)
    backward = jnp.einsum('rjd,jkfd->rjkf', grad_blocks, out_blocks).reshape(row_count, NB2, BLK)
    labels = jnp.arange(FB, dtype=jnp.int32)
    gather_matrix = (read_blocks[:, None] == labels[None, :]).astype(jnp.float32)
    grad_hidden = jnp.einsum('rmf,mb->rbf', backward, gather_matrix, precision=lax.Precision.HIGHEST)
    _, pullback = jax.vjp(jax.nn.gelu, pre_hidden)
    grad_pre = pullback(grad_hidden)[0].astype(jnp.bfloat16)
    grad_weight_in = jnp.einsum('rbi,rbo->bio', picked.astype(jnp.float32), grad_pre.astype(jnp.float32))
    grad_picked = jnp.einsum('rbo,bio->rbi', grad_pre.astype(jnp.float32), weight_in.astype(jnp.float32))
    input_labels = jnp.arange(DB, dtype=jnp.int32)
    fold_matrix = (rows_in[:, None] == input_labels[None, :]).astype(jnp.float32)
    grad_normed = jnp.einsum('rbi,bj->rji', grad_picked, fold_matrix, precision=lax.Precision.HIGHEST)
    return (grad_normed.reshape(row_count, D).astype(jnp.bfloat16), grad_weight_in, grad_weight_out)

def reference(patches, teacher, route, gates, w_in, in_rows, in_cols, w_out, out_rows):
    features = patches.astype(jnp.float32)
    normed = normalize(features).astype(jnp.bfloat16)
    group_size = N_EXPERT * TOK_DEV
    expert_of = route[:, 0]
    experts_all = jnp.arange(EXPERTS, dtype=jnp.int32)
    lane_index = jnp.arange(ROWB, dtype=jnp.int32)

    def group_plan(group_index):
        first_row = group_index * group_size
        expert_keys = lax.dynamic_slice_in_dim(expert_of, first_row, group_size)
        row_order = jnp.argsort(expert_keys, stable=True).astype(jnp.int32) + first_row
        row_order = jnp.concatenate([row_order, jnp.full((ROWB,), TOKENS, jnp.int32)])
        counts = lax.optimization_barrier(jnp.sum((expert_keys[:, None] == experts_all[None, :]).astype(jnp.int32), axis=0))
        firsts = jnp.cumsum(counts) - counts
        return (row_order, counts, firsts)

    def block_rows(row_order, counts, firsts, expert_index, block_index):
        block_start = (firsts[expert_index] + block_index * ROWB).astype(jnp.int32)
        chosen = lax.dynamic_slice_in_dim(row_order, block_start, ROWB)
        is_live = block_index * ROWB + lane_index < counts[expert_index]
        return jnp.where(is_live, chosen, TOKENS).astype(jnp.int32)

    def forward_group(group_index, combined):
        row_order, counts, firsts = group_plan(group_index)

        def forward_expert(expert_index, combined):
            read_blocks = hidden_order(in_cols[expert_index])[out_rows[expert_index]]
            block_total = (counts[expert_index] + ROWB - 1) // ROWB

            def forward_block(block_index, combined):
                chosen = block_rows(row_order, counts, firsts, expert_index, block_index)
                normed_rows = jnp.take(normed, chosen, axis=0, mode='fill', fill_value=0)
                picked, pre_hidden, spread = expert_hidden(normed_rows, w_in[expert_index], in_rows[expert_index], read_blocks)
                produced = expert_output(spread, w_out[expert_index]).astype(jnp.bfloat16)
                return combined.at[chosen].set(produced, mode='drop')
            return lax.fori_loop(0, block_total, forward_block, combined)
        return lax.fori_loop(0, EXPERTS, forward_expert, combined)
    combined = lax.fori_loop(0, N_DP, forward_group, jnp.zeros((TOKENS, D), jnp.bfloat16))
    gate_rows = gates.astype(jnp.float32)[:, None]
    summed = features + gate_rows * combined.astype(jnp.float32)
    student = summed.astype(jnp.bfloat16)
    mismatch = summed - teacher.astype(jnp.float32)
    grad_expert = (gate_rows * mismatch).astype(jnp.bfloat16)

    def backward_group(group_index, running):
        row_order, counts, firsts = group_plan(group_index)

        def backward_expert(expert_index, running):
            read_blocks = hidden_order(in_cols[expert_index])[out_rows[expert_index]]
            block_total = (counts[expert_index] + ROWB - 1) // ROWB

            def backward_block(block_index, running):
                grad_rows, grad_in, grad_out = running
                chosen = block_rows(row_order, counts, firsts, expert_index, block_index)
                normed_rows = jnp.take(normed, chosen, axis=0, mode='fill', fill_value=0)
                grad_out_rows = jnp.take(grad_expert, chosen, axis=0, mode='fill', fill_value=0)
                picked, pre_hidden, spread = expert_hidden(normed_rows, w_in[expert_index], in_rows[expert_index], read_blocks)
                grad_normed, part_in, part_out = expert_backward(grad_out_rows, picked, pre_hidden, spread, w_in[expert_index], in_rows[expert_index], w_out[expert_index], read_blocks)
                return (grad_rows.at[chosen].set(grad_normed, mode='drop'), grad_in.at[expert_index].add(part_in), grad_out.at[expert_index].add(part_out))
            return lax.fori_loop(0, block_total, backward_block, running)
        return lax.fori_loop(0, EXPERTS, backward_expert, running)
    initial = (jnp.zeros((TOKENS, D), jnp.bfloat16), jnp.zeros((EXPERTS, FB, BLK, BLK), jnp.float32), jnp.zeros((EXPERTS, NB2, BLK, BLK), jnp.float32))
    grad_rows, grad_in, grad_out = lax.fori_loop(0, N_DP, backward_group, initial)
    _, pullback = jax.vjp(normalize, features)
    grad_patches = mismatch + pullback(grad_rows.astype(jnp.float32))[0]
    return (student, grad_patches, grad_in, grad_out)
```

```python
import jax
import jax.numpy as jnp
from jax import lax
from jax.experimental import pallas as pl
from jax.experimental.pallas import tpu as pltpu
from jax.sharding import PartitionSpec as P

BLK = 128
K2 = 4
DB = 10
FB = 40
D = DB * BLK
SLOT = 8
EPS = 1e-06
GELU_K = 0.7978845608028654
GELU_C = 0.044715
F32 = jnp.float32
BF16 = jnp.bfloat16
NT = (((1,), (1,)), ((), ()))


def dot(a, b):
    return jnp.dot(a, b, preferred_element_type=F32)


def dot_nt(a, b):
    return lax.dot_general(a, b, NT, preferred_element_type=F32)


def slot_matrix(route_row, owners):
    rows = route_row.shape[1]
    slots = owners * SLOT
    expert = lax.broadcasted_iota(jnp.int32, (owners, rows), 0)
    hits = expert == route_row
    first = lax.broadcasted_iota(jnp.int32, (rows, rows), 0)
    second = lax.broadcasted_iota(jnp.int32, (rows, rows), 1)
    before = dot(hits.astype(BF16), (first < second).astype(BF16))
    rank = jnp.sum(jnp.where(hits, before, 0.0), axis=0, keepdims=True).astype(jnp.int32)
    slot_row = route_row * SLOT + rank
    slot = lax.broadcasted_iota(jnp.int32, (slots, rows), 0)
    return slot == slot_row


def pack_kernel(route_ref, gates_ref, patches_ref, teacher_ref, out_ref):
    owners = out_ref.shape[0] // SLOT
    place = slot_matrix(route_ref[...], owners)
    one_hot = place.astype(BF16)
    out_ref[:, :D] = dot(one_hot, patches_ref[...]).astype(BF16)
    out_ref[:, D : 2 * D] = dot(one_hot, teacher_ref[...]).astype(BF16)
    gates = jnp.broadcast_to(gates_ref[...].astype(F32), place.shape)
    gate = jnp.sum(jnp.where(place, gates, 0.0), axis=1, keepdims=True)
    out_ref[:, 2 * D :] = jnp.broadcast_to(gate, (place.shape[0], BLK)).astype(BF16)


def expert_kernel(
    in_rows,
    in_cols,
    out_rows,
    where_ref,
    pay_ref,
    w_in_ref,
    w_out_ref,
    ret_ref,
    *rest,
):
    n_x = len(rest) - 9
    parts = rest[:n_x]
    xn, xnt, hid, slope, gh, gn, grads, gate, sems = rest[n_x:]
    share = FB // n_x
    half = share // 2
    my_x, my_y = where_ref[0], where_ref[1]

    def place(block, kind):
        x = block // share
        y = (block % share) // half
        rel_x = lax.rem(x - my_x + n_x, n_x)
        rel_y = lax.rem(y - my_y + 2, 2)
        return rel_x, rel_y * share + kind * half + block % half

    feats = pay_ref[:, :D].astype(F32)
    centred = feats - jnp.mean(feats, axis=-1, keepdims=True)
    variance = jnp.mean(centred * centred, axis=-1, keepdims=True)
    normed = centred * lax.rsqrt(variance + EPS)
    for i in range(DB):
        piece = normed[:, i * BLK : (i + 1) * BLK]
        xn[i] = piece.astype(BF16)
        xnt[i] = piece.T.astype(BF16)
    gn[...] = jnp.zeros_like(gn)
    gate[...] = pay_ref[:, 2 * D :].astype(F32)

    def forward(step, carry):
        for q in range(4):
            b = step * 4 + q
            c = in_cols[b]
            v = dot(xn[in_rows[b]], w_in_ref[b])
            v2 = v * v
            t = jnp.tanh(GELU_K * v * (1.0 + GELU_C * v2))
            half_p = 0.5 + 0.5 * t
            hid[c] = (v * half_p).astype(BF16)
            slope[c] = half_p + (0.5 * GELU_K) * v * (1.0 - t * t) * (1.0 + (3.0 * GELU_C) * v2)
            gh[c] = jnp.zeros_like(v)
        return carry

    lax.fori_loop(0, FB // 4, forward, 0)

    for j in range(DB):
        lanes = slice(j * BLK, (j + 1) * BLK)
        reads = [out_rows[K2 * j + k] for k in range(K2)]
        spread = jnp.concatenate([hid[r] for r in reads], axis=1)
        weight = w_out_ref[K2 * j : K2 * (j + 1)].reshape(K2 * BLK, BLK)
        produced = dot(spread, weight).astype(BF16)
        ret_ref[:, lanes] = produced
        g = gate[...]
        summed = pay_ref[:, lanes].astype(F32) + g * produced.astype(F32)
        mismatch = summed - pay_ref[:, D + j * BLK : D + (j + 1) * BLK].astype(F32)
        grad = g * mismatch
        grad_b = grad.astype(BF16)
        grad_t = grad.T.astype(BF16)
        outer = dot(grad_t, spread)
        back = dot_nt(grad_b, weight)
        for k in range(K2):
            rel_x, pos = place(K2 * j + k, 1)
            grads[rel_x, pos] = outer[:, k * BLK : (k + 1) * BLK].astype(BF16)
            gh[reads[k]] += back[:, k * BLK : (k + 1) * BLK]

    def backward(step, carry):
        for q in range(4):
            b = step * 4 + q
            c = in_cols[b]
            i = in_rows[b]
            grad_pre = (gh[c] * slope[c]).astype(BF16)
            rel_x, pos = place(b, 0)
            grads[rel_x, pos] = dot(xnt[i], grad_pre).astype(BF16)
            gn[i] += dot_nt(grad_pre, w_in_ref[b])
        return carry

    lax.fori_loop(0, FB // 4, backward, 0)

    copies = [
        pltpu.make_async_copy(grads.at[k], part, sems.at[k]) for k, part in enumerate(parts)
    ]
    for copy in copies:
        copy.start()
    for i in range(DB):
        ret_ref[:, D + i * BLK : D + (i + 1) * BLK] = gn[i].astype(BF16)
    for copy in copies:
        copy.wait()


def finish_kernel(route_ref, gates_ref, patches_ref, teacher_ref, ret_ref, student_ref, grad_ref):
    owners = ret_ref.shape[0] // SLOT
    place = slot_matrix(route_ref[...], owners).astype(F32)
    pick = place.T
    gates = gates_ref[...].astype(F32)
    gated = jnp.broadcast_to(gates, place.shape) * place
    gate = jnp.sum(gated.T, axis=1, keepdims=True)
    pick = pick.astype(BF16)
    feats = patches_ref[...].astype(F32)
    summed = feats + gate * dot(pick, ret_ref[:, :D])
    student_ref[...] = summed.astype(BF16)
    mismatch = summed - teacher_ref[...].astype(F32)
    grad = dot(pick, ret_ref[:, D:])
    centred = feats - jnp.mean(feats, axis=-1, keepdims=True)
    variance = jnp.mean(centred * centred, axis=-1, keepdims=True)
    scale = lax.rsqrt(variance + EPS)
    normed = centred * scale
    mean_grad = jnp.mean(grad, axis=-1, keepdims=True)
    mean_both = jnp.mean(grad * normed, axis=-1, keepdims=True)
    grad_ref[...] = mismatch + scale * (grad - mean_grad - normed * mean_both)


def shift(n_x, dx, dy):
    return [
        (x * 2 + y, ((x + dx) % n_x) * 2 + (y + dy) % 2) for x in range(n_x) for y in range(2)
    ]


VMEM_SPEC = pl.BlockSpec(memory_space=pltpu.VMEM)
SMEM_SPEC = pl.BlockSpec(memory_space=pltpu.SMEM)
ANY_SPEC = pl.BlockSpec(memory_space=pl.ANY)


def local(patches, teacher, route, gates, w_in, in_rows, in_cols, w_out, out_rows):
    rows = patches.shape[0]
    owners = lax.axis_size("expert")
    n_x = lax.axis_size("dp") // 2
    slots = owners * SLOT
    share = FB // n_x
    route_row = route.reshape(1, rows)
    gates_row = gates.reshape(1, rows)
    payload = pl.pallas_call(
        pack_kernel,
        out_shape=jax.ShapeDtypeStruct((slots, 2 * D + BLK), BF16),
        in_specs=[VMEM_SPEC] * 4,
        out_specs=VMEM_SPEC,
        compiler_params=pltpu.CompilerParams(vmem_limit_bytes=16 << 20),
        name="pack",
    )(route_row, gates_row, patches, teacher)

    def exchange(values):
        width = values.shape[1]
        blocks = values.reshape(owners, SLOT, width)
        out = lax.all_to_all(blocks, "expert", split_axis=0, concat_axis=0, tiled=True)
        return out.reshape(slots, width)

    arrived = exchange(payload)
    me = lax.axis_index("dp")
    where = jnp.stack([me // 2, me % 2]).astype(jnp.int32)
    part = jax.ShapeDtypeStruct((2 * share, BLK, BLK), BF16)
    returned, *parts = pl.pallas_call(
        expert_kernel,
        out_shape=(jax.ShapeDtypeStruct((slots, 2 * D), BF16),) + (part,) * n_x,
        in_specs=[SMEM_SPEC] * 4 + [VMEM_SPEC] * 3,
        out_specs=(VMEM_SPEC,) + (ANY_SPEC,) * n_x,
        scratch_shapes=[
            pltpu.VMEM((DB, slots, BLK), BF16),
            pltpu.VMEM((DB, BLK, slots), BF16),
            pltpu.VMEM((FB, slots, BLK), BF16),
            pltpu.VMEM((FB, slots, BLK), F32),
            pltpu.VMEM((FB, slots, BLK), F32),
            pltpu.VMEM((DB, slots, BLK), F32),
            pltpu.VMEM((n_x, 2 * share, BLK, BLK), BF16),
            pltpu.VMEM((slots, BLK), F32),
            pltpu.SemaphoreType.DMA((n_x,)),
        ],
        compiler_params=pltpu.CompilerParams(vmem_limit_bytes=44 << 20),
        name="expert",
    )(in_rows[0], in_cols[0], out_rows[0], where, arrived, w_in[0], w_out[0])

    back = exchange(returned)
    total = parts[0].astype(F32)
    for dx in (2, 1, 3):
        total = total + lax.ppermute(parts[dx], "dp", shift(n_x, dx, 0)).astype(F32)
    other = lax.ppermute(total[share:].astype(BF16), "dp", shift(n_x, 0, 1))
    total = total[:share] + other.astype(F32)
    half = share // 2
    part_in = total[:half]
    part_out = jnp.swapaxes(total[half:], 1, 2)

    student, grad_patches = pl.pallas_call(
        finish_kernel,
        out_shape=(
            jax.ShapeDtypeStruct((rows, D), BF16),
            jax.ShapeDtypeStruct((rows, D), F32),
        ),
        in_specs=[VMEM_SPEC] * 5,
        out_specs=(VMEM_SPEC, VMEM_SPEC),
        compiler_params=pltpu.CompilerParams(vmem_limit_bytes=16 << 20),
        name="finish",
    )(route_row, gates_row, patches, teacher, back)
    return (student, grad_patches, part_in[None], part_out[None])


def solution(mesh):
    placed = (
        P(("dp", "expert"), None),
        P(("dp", "expert"), None),
        P(("dp", "expert"), None),
        P(("dp", "expert")),
        P("expert", None, None, None),
        P("expert", None),
        P("expert", None),
        P("expert", None, None, None),
        P("expert", None),
    )
    return jax.shard_map(
        local,
        mesh=mesh,
        in_specs=placed,
        out_specs=(
            P(("dp", "expert"), None),
            P(("dp", "expert"), None),
            P("expert", "dp", None, None),
            P("expert", "dp", None, None),
        ),
        check_vma=False,
    )
```

```python
import jax
import jax.numpy as jnp
from jax import lax
from jax.experimental import pallas as pl
from jax.experimental.pallas import tpu as pltpu
from jax.sharding import PartitionSpec as P

BLK = 128
K2 = 4
DB = 10
FB = 40
D = DB * BLK
SLOT = 8
EPS = 1e-06
GELU_K = 0.7978845608028654
GELU_C = 0.044715
F32 = jnp.float32
BF16 = jnp.bfloat16
NT = (((1,), (1,)), ((), ()))


def dot(a, b):
    return jnp.dot(a, b, preferred_element_type=F32)


def dot_nt(a, b):
    return lax.dot_general(a, b, NT, preferred_element_type=F32)


def slot_matrix(route_row, owners):
    rows = route_row.shape[1]
    slots = owners * SLOT
    expert = lax.broadcasted_iota(jnp.int32, (owners, rows), 0)
    hits = expert == route_row
    first = lax.broadcasted_iota(jnp.int32, (rows, rows), 0)
    second = lax.broadcasted_iota(jnp.int32, (rows, rows), 1)
    before = dot(hits.astype(BF16), (first < second).astype(BF16))
    rank = jnp.sum(jnp.where(hits, before, 0.0), axis=0, keepdims=True).astype(jnp.int32)
    slot_row = route_row * SLOT + rank
    slot = lax.broadcasted_iota(jnp.int32, (slots, rows), 0)
    return slot == slot_row


def layer_norm(feats):
    centred = feats - jnp.mean(feats, axis=-1, keepdims=True)
    variance = jnp.mean(centred * centred, axis=-1, keepdims=True)
    scale = lax.rsqrt(variance + EPS)
    return centred * scale, scale


def pack_kernel(route_ref, gates_ref, patches_hbm, teacher_hbm, out_hbm, patches, teacher, out, sems):
    loads = [
        pltpu.make_async_copy(patches_hbm, patches, sems.at[0]),
        pltpu.make_async_copy(teacher_hbm, teacher, sems.at[1]),
    ]
    for load in loads:
        load.start()
    owners = out.shape[0] // SLOT
    place = slot_matrix(route_ref[...], owners)
    one_hot = place.astype(BF16)
    gates = gates_ref[...].astype(F32)
    gate = jnp.sum(jnp.where(place, gates, 0.0), axis=1, keepdims=True)
    out[:, 2 * D :] = jnp.broadcast_to(gate, (place.shape[0], BLK)).astype(BF16)
    loads[0].wait()
    feats = patches[...].astype(F32)
    normed, _ = layer_norm(feats)
    out[:, :D] = dot(one_hot, normed.astype(BF16)).astype(BF16)
    loads[1].wait()
    differ = (feats - teacher[...].astype(F32)).astype(BF16)
    out[:, D : 2 * D] = (gate * dot(one_hot, differ)).astype(BF16)
    store = pltpu.make_async_copy(out, out_hbm, sems.at[2])
    store.start()
    store.wait()


def expert_kernel(
    in_rows,
    in_cols,
    out_rows,
    where_ref,
    pay_ref,
    w_in_ref,
    w_out_hbm,
    ret_hbm,
    *rest,
):
    n_x = len(rest) // 2 - 6
    parts = (rest[:n_x], rest[n_x : 2 * n_x])
    w_out_ref, ret, xnt, hid, slope, gh, gn, grads, gate, load_sem, ret_sems, sems = rest[2 * n_x :]
    share = FB // n_x
    half = share // 2
    my_x, my_y = where_ref[0], where_ref[1]
    load = pltpu.make_async_copy(w_out_hbm, w_out_ref, load_sem.at[0])
    load.start()

    def place(block):
        x = block // share
        y = (block % share) // half
        return lax.rem(x - my_x + n_x, n_x), lax.rem(y - my_y + 2, 2) * half + block % half

    def send(kind):
        copies = [
            pltpu.make_async_copy(grads.at[kind, x], parts[kind][x], sems.at[kind, x])
            for x in range(n_x)
        ]
        copies.append(
            pltpu.make_async_copy(
                ret.at[:, pl.ds((1 - kind) * D, D)],
                ret_hbm.at[:, pl.ds((1 - kind) * D, D)],
                ret_sems.at[kind],
            )
        )
        for copy in copies:
            copy.start()
        return copies

    for i in range(DB):
        xnt[i] = pay_ref[:, i * BLK : (i + 1) * BLK].T
    gn[...] = jnp.zeros_like(gn)
    gate[...] = jnp.square(pay_ref[:, 2 * D :].astype(F32))

    def forward(step, carry):
        for q in range(4):
            b = step * 4 + q
            c = in_cols[b]
            lanes = pl.ds(pl.multiple_of(in_rows[b] * BLK, BLK), BLK)
            v = dot(pay_ref[:, lanes], w_in_ref[b])
            v2 = v * v
            t = jnp.tanh(v * (GELU_K + (GELU_K * GELU_C) * v2))
            half_p = 0.5 + 0.5 * t
            hid[c] = (v * half_p).astype(BF16)
            slope[c] = half_p + v * (1.0 - t * t) * (
                0.5 * GELU_K + (1.5 * GELU_K * GELU_C) * v2
            )
            gh[c] = jnp.zeros_like(v)
        return carry

    lax.fori_loop(0, FB // 4, forward, 0)
    load.wait()

    for j in range(DB):
        lanes = slice(j * BLK, (j + 1) * BLK)
        reads = [out_rows[K2 * j + k] for k in range(K2)]
        spread = jnp.concatenate([hid[r] for r in reads], axis=1)
        weight = w_out_ref[K2 * j : K2 * (j + 1)].reshape(K2 * BLK, BLK)
        produced = dot(spread, weight).astype(BF16)
        ret[:, lanes] = produced
        grad = pay_ref[:, D + j * BLK : D + (j + 1) * BLK].astype(F32) + gate[
            ...
        ] * produced.astype(F32)
        grad_b = grad.astype(BF16)
        outer = dot(grad_b.T, spread)
        back = dot_nt(grad_b, weight)
        for k in range(K2):
            rel_x, pos = place(K2 * j + k)
            grads[1, rel_x, pos] = outer[:, k * BLK : (k + 1) * BLK].astype(BF16)
            gh[reads[k]] += back[:, k * BLK : (k + 1) * BLK]

    copies = send(1)

    def backward(step, carry):
        for q in range(4):
            b = step * 4 + q
            c = in_cols[b]
            i = in_rows[b]
            grad_pre = (gh[c] * slope[c]).astype(BF16)
            rel_x, pos = place(b)
            grads[0, rel_x, pos] = dot(xnt[i], grad_pre).astype(BF16)
            gn[i] += dot_nt(grad_pre, w_in_ref[b])
        return carry

    lax.fori_loop(0, FB // 4, backward, 0)
    for i in range(DB):
        ret[:, D + i * BLK : D + (i + 1) * BLK] = gn[i].astype(BF16)
    copies += send(0)
    for copy in copies:
        copy.wait()


def finish_kernel(route_ref, gates_ref, patches_ref, teacher_ref, ret_ref, student_ref, grad_ref):
    owners = ret_ref.shape[0] // SLOT
    place = slot_matrix(route_ref[...], owners).astype(F32)
    pick = place.T
    gates = gates_ref[...].astype(F32)
    gated = jnp.broadcast_to(gates, place.shape) * place
    gate = jnp.sum(gated.T, axis=1, keepdims=True)
    pick = pick.astype(BF16)
    feats = patches_ref[...].astype(F32)
    summed = feats + gate * dot(pick, ret_ref[:, :D])
    student_ref[...] = summed.astype(BF16)
    mismatch = summed - teacher_ref[...].astype(F32)
    grad = dot(pick, ret_ref[:, D:])
    normed, scale = layer_norm(feats)
    mean_grad = jnp.mean(grad, axis=-1, keepdims=True)
    mean_both = jnp.mean(grad * normed, axis=-1, keepdims=True)
    grad_ref[...] = mismatch + scale * (grad - mean_grad - normed * mean_both)


def total_kernel(mine_in_ref, mine_out_ref, other_ref, in_ref, out_ref):
    half = in_ref.shape[0]
    for q in range(half):
        in_ref[q] = mine_in_ref[q] + other_ref[q].astype(F32)
        out_ref[q] = (mine_out_ref[q] + other_ref[half + q].astype(F32)).T


def shift(n_x, dx, dy):
    return [
        (x * 2 + y, ((x + dx) % n_x) * 2 + (y + dy) % 2) for x in range(n_x) for y in range(2)
    ]


VMEM_SPEC = pl.BlockSpec(memory_space=pltpu.VMEM)
SMEM_SPEC = pl.BlockSpec(memory_space=pltpu.SMEM)
HBM_SPEC = pl.BlockSpec(memory_space=pltpu.HBM)


def local(patches, teacher, route, gates, w_in, in_rows, in_cols, w_out, out_rows):
    rows = patches.shape[0]
    owners = lax.axis_size("expert")
    n_x = lax.axis_size("dp") // 2
    slots = owners * SLOT
    share = FB // n_x
    route_row = route.reshape(1, rows)
    gates_row = gates.reshape(1, rows)
    payload = pl.pallas_call(
        pack_kernel,
        out_shape=jax.ShapeDtypeStruct((slots, 2 * D + BLK), BF16),
        in_specs=[VMEM_SPEC] * 2 + [HBM_SPEC] * 2,
        out_specs=HBM_SPEC,
        scratch_shapes=[
            pltpu.VMEM((rows, D), BF16),
            pltpu.VMEM((rows, D), BF16),
            pltpu.VMEM((slots, 2 * D + BLK), BF16),
            pltpu.SemaphoreType.DMA((3,)),
        ],
        compiler_params=pltpu.CompilerParams(vmem_limit_bytes=60 << 20),
        name="pack",
    )(route_row, gates_row, patches, teacher)

    def exchange(values):
        width = values.shape[1]
        blocks = values.reshape(owners, SLOT, width)
        out = lax.all_to_all(blocks, "expert", split_axis=0, concat_axis=0, tiled=True)
        return out.reshape(slots, width)

    arrived = exchange(payload)
    me = lax.axis_index("dp")
    where = jnp.stack([me // 2, me % 2]).astype(jnp.int32)
    part = jax.ShapeDtypeStruct((share, BLK, BLK), BF16)
    returned, *parts = pl.pallas_call(
        expert_kernel,
        out_shape=(jax.ShapeDtypeStruct((slots, 2 * D), BF16),) + (part,) * (2 * n_x),
        in_specs=[SMEM_SPEC] * 4 + [VMEM_SPEC] * 2 + [HBM_SPEC],
        out_specs=(HBM_SPEC,) * (1 + 2 * n_x),
        scratch_shapes=[
            pltpu.VMEM((FB, BLK, BLK), BF16),
            pltpu.VMEM((slots, 2 * D), BF16),
            pltpu.VMEM((DB, BLK, slots), BF16),
            pltpu.VMEM((FB, slots, BLK), BF16),
            pltpu.VMEM((FB, slots, BLK), F32),
            pltpu.VMEM((FB, slots, BLK), F32),
            pltpu.VMEM((DB, slots, BLK), F32),
            pltpu.VMEM((2, n_x, share, BLK, BLK), BF16),
            pltpu.VMEM((slots, BLK), F32),
            pltpu.SemaphoreType.DMA((1,)),
            pltpu.SemaphoreType.DMA((2,)),
            pltpu.SemaphoreType.DMA((2, n_x)),
        ],
        compiler_params=pltpu.CompilerParams(vmem_limit_bytes=60 << 20),
        name="expert",
    )(in_rows[0], in_cols[0], out_rows[0], where, arrived, w_in[0], w_out[0])
    part_in, part_out = parts[:n_x], parts[n_x:]

    back = exchange(returned)
    half = share // 2

    def pass_on(values, dx, dy=0):
        return lax.ppermute(values, "dp", shift(n_x, dx, dy))

    def add(*values):
        return sum(v.astype(F32) for v in values)

    far_in = pass_on(part_in[2], 1)
    far_out = pass_on(part_out[2], 3)
    near_out = pass_on(part_out[1], 1)
    near_in = pass_on(part_in[3], 3)
    pair_in = pass_on(add(part_in[1], far_in).astype(BF16), 1)
    pair_out = pass_on(add(part_out[3], far_out).astype(BF16), 3)
    total_in = add(part_in[0], near_in, pair_in)
    total_out = add(part_out[0], near_out, pair_out)
    other = pass_on(jnp.concatenate([total_in[half:], total_out[half:]]).astype(BF16), 0, 1)
    block = jax.ShapeDtypeStruct((half, BLK, BLK), F32)
    grad_in, grad_out = pl.pallas_call(
        total_kernel,
        out_shape=(block, block),
        in_specs=[VMEM_SPEC] * 3,
        out_specs=(VMEM_SPEC, VMEM_SPEC),
        compiler_params=pltpu.CompilerParams(vmem_limit_bytes=16 << 20),
        name="total",
    )(total_in[:half], total_out[:half], other)

    student, grad_patches = pl.pallas_call(
        finish_kernel,
        out_shape=(
            jax.ShapeDtypeStruct((rows, D), BF16),
            jax.ShapeDtypeStruct((rows, D), F32),
        ),
        in_specs=[VMEM_SPEC] * 5,
        out_specs=(VMEM_SPEC, VMEM_SPEC),
        compiler_params=pltpu.CompilerParams(vmem_limit_bytes=16 << 20),
        name="finish",
    )(route_row, gates_row, patches, teacher, back)
    return (student, grad_patches, grad_in[None], grad_out[None])


def solution(mesh):
    placed = (
        P(("dp", "expert"), None),
        P(("dp", "expert"), None),
        P(("dp", "expert"), None),
        P(("dp", "expert")),
        P("expert", None, None, None),
        P("expert", None),
        P("expert", None),
        P("expert", None, None, None),
        P("expert", None),
    )
    return jax.shard_map(
        local,
        mesh=mesh,
        in_specs=placed,
        out_specs=(
            P(("dp", "expert"), None),
            P(("dp", "expert"), None),
            P("expert", "dp", None, None),
            P("expert", "dp", None, None),
        ),
        check_vma=False,
    )
```

```python
import jax
import jax.numpy as jnp
from jax import lax
from jax.experimental import pallas as pl
from jax.experimental.pallas import tpu as pltpu
from jax.sharding import PartitionSpec as P

BLK = 128
K2 = 4
DB = 10
FB = 40
D = DB * BLK
SLOT = 8
UNROLL = 20
EPS = 1e-06
GELU_K = 0.7978845608028654
GELU_C = 0.044715
F32 = jnp.float32
BF16 = jnp.bfloat16
NT = (((1,), (1,)), ((), ()))


def dot(a, b):
    return jnp.dot(a, b, preferred_element_type=F32)


def dot_nt(a, b):
    return lax.dot_general(a, b, NT, preferred_element_type=F32)


def slot_matrix(route_row, owners):
    rows = route_row.shape[1]
    slots = owners * SLOT
    expert = lax.broadcasted_iota(jnp.int32, (owners, rows), 0)
    hits = expert == route_row
    first = lax.broadcasted_iota(jnp.int32, (rows, rows), 0)
    second = lax.broadcasted_iota(jnp.int32, (rows, rows), 1)
    before = dot(hits.astype(BF16), (first < second).astype(BF16))
    rank = jnp.sum(jnp.where(hits, before, 0.0), axis=0, keepdims=True).astype(jnp.int32)
    slot_row = route_row * SLOT + rank
    slot = lax.broadcasted_iota(jnp.int32, (slots, rows), 0)
    return slot == slot_row


def layer_norm(feats):
    centred = feats - jnp.mean(feats, axis=-1, keepdims=True)
    variance = jnp.mean(centred * centred, axis=-1, keepdims=True)
    scale = lax.rsqrt(variance + EPS)
    return centred * scale, scale


def pack_kernel(route_ref, gates_ref, patches_hbm, teacher_hbm, out_hbm, patches, teacher, out, sems):
    loads = [
        pltpu.make_async_copy(patches_hbm, patches, sems.at[0]),
        pltpu.make_async_copy(teacher_hbm, teacher, sems.at[1]),
    ]
    for load in loads:
        load.start()

    def store(second):
        lanes = pl.ds(second * D, D + second * BLK)
        return pltpu.make_async_copy(out.at[:, lanes], out_hbm.at[:, lanes], sems.at[2 + second])

    owners = out.shape[0] // SLOT
    place = slot_matrix(route_ref[...], owners)
    one_hot = place.astype(BF16)
    gates = gates_ref[...].astype(F32)
    gate = jnp.sum(jnp.where(place, gates, 0.0), axis=1, keepdims=True)
    out[:, 2 * D :] = jnp.broadcast_to(gate, (place.shape[0], BLK)).astype(BF16)
    loads[0].wait()
    feats = patches[...].astype(F32)
    normed, _ = layer_norm(feats)
    out[:, :D] = dot(one_hot, normed.astype(BF16)).astype(BF16)
    early = store(0)
    early.start()
    loads[1].wait()
    differ = (feats - teacher[...].astype(F32)).astype(BF16)
    out[:, D : 2 * D] = (gate * dot(one_hot, differ)).astype(BF16)
    late = store(1)
    late.start()
    early.wait()
    late.wait()


def expert_kernel(
    in_rows,
    in_cols,
    out_rows,
    where_ref,
    pay_hbm,
    w_in_ref,
    w_out_hbm,
    ret_hbm,
    *rest,
):
    n_x = (len(rest) - 15) // 2
    parts = (rest[:n_x], rest[n_x : 2 * n_x])
    pay_ref, w_out_ref, ret, xnt, hid, slope, gh, gn, grads, gate, ge, get, load_sem, ret_sems, sems = rest[2 * n_x :]
    share = FB // n_x
    half = share // 2
    my_x, my_y = where_ref[0], where_ref[1]
    first, rest_of = pl.ds(0, D), pl.ds(D, D + BLK)
    loads = [
        pltpu.make_async_copy(pay_hbm.at[:, first], pay_ref.at[:, first], load_sem.at[0]),
        pltpu.make_async_copy(pay_hbm.at[:, rest_of], pay_ref.at[:, rest_of], load_sem.at[1]),
        pltpu.make_async_copy(w_out_hbm, w_out_ref, load_sem.at[2]),
    ]
    for load in loads:
        load.start()

    def place(block):
        x = block // share
        y = (block % share) // half
        return lax.rem(x - my_x + n_x, n_x), lax.rem(y - my_y + 2, 2) * half + block % half

    def send(kind):
        copies = [
            pltpu.make_async_copy(grads.at[kind, x], parts[kind][x], sems.at[kind, x])
            for x in range(n_x)
        ]
        copies.append(
            pltpu.make_async_copy(
                ret.at[:, pl.ds((1 - kind) * D, D)],
                ret_hbm.at[:, pl.ds((1 - kind) * D, D)],
                ret_sems.at[kind],
            )
        )
        for copy in copies:
            copy.start()
        return copies

    gn[...] = jnp.zeros_like(gn)
    loads[0].wait()
    for i in range(DB):
        xnt[i] = pay_ref[:, i * BLK : (i + 1) * BLK].T

    def forward(step, carry):
        for q in range(UNROLL):
            b = step * UNROLL + q
            c = in_cols[b]
            lanes = pl.ds(pl.multiple_of(in_rows[b] * BLK, BLK), BLK)
            v = dot(pay_ref[:, lanes], w_in_ref[b])
            v2 = v * v
            t = jnp.tanh(v * (GELU_K + (GELU_K * GELU_C) * v2))
            half_p = 0.5 + 0.5 * t
            hid[c] = (v * half_p).astype(BF16)
            slope[c] = half_p + v * (1.0 - t * t) * (
                0.5 * GELU_K + (1.5 * GELU_K * GELU_C) * v2
            )
            gh[c] = jnp.zeros_like(v)
        return carry

    lax.fori_loop(0, FB // UNROLL, forward, 0)
    loads[1].wait()
    loads[2].wait()
    gate[...] = jnp.square(pay_ref[:, 2 * D :].astype(F32))

    def read(j):
        return [out_rows[K2 * j + k] for k in range(K2)]

    def spread(j):
        return jnp.concatenate([hid[r] for r in read(j)], axis=1)

    def weight(j):
        return w_out_ref[K2 * j : K2 * (j + 1)].reshape(K2 * BLK, BLK)

    for j in range(DB):
        produced = dot(spread(j), weight(j)).astype(BF16)
        ret[:, j * BLK : (j + 1) * BLK] = produced
        given = pay_ref[:, D + j * BLK : D + (j + 1) * BLK].astype(F32)
        grad = (given + gate[...] * produced.astype(F32)).astype(BF16)
        ge[j] = grad
        get[j] = grad.T
    for j in range(DB):
        outer = dot(get[j], spread(j))
        back = dot_nt(ge[j], weight(j))
        for k, r in enumerate(read(j)):
            rel_x, pos = place(K2 * j + k)
            grads[1, rel_x, pos] = outer[:, k * BLK : (k + 1) * BLK].astype(BF16)
            gh[r] += back[:, k * BLK : (k + 1) * BLK]

    copies = send(1)

    def backward(step, carry):
        for q in range(UNROLL):
            b = step * UNROLL + q
            c = in_cols[b]
            i = in_rows[b]
            grad_pre = (gh[c] * slope[c]).astype(BF16)
            rel_x, pos = place(b)
            grads[0, rel_x, pos] = dot(xnt[i], grad_pre).astype(BF16)
            gn[i] += dot_nt(grad_pre, w_in_ref[b])
        return carry

    lax.fori_loop(0, FB // UNROLL, backward, 0)
    for i in range(DB):
        ret[:, D + i * BLK : D + (i + 1) * BLK] = gn[i].astype(BF16)
    copies += send(0)
    for copy in copies:
        copy.wait()


def finish_kernel(route_ref, gates_ref, patches_ref, teacher_ref, ret_ref, student_ref, grad_ref, corner_ref):
    owners = ret_ref.shape[0] // SLOT
    place = slot_matrix(route_ref[...], owners).astype(F32)
    pick = place.T
    gates = gates_ref[...].astype(F32)
    gated = jnp.broadcast_to(gates, place.shape) * place
    gate = jnp.sum(gated.T, axis=1, keepdims=True)
    pick = pick.astype(BF16)
    feats = patches_ref[...].astype(F32)
    summed = feats + gate * dot(pick, ret_ref[:, :D])
    student_ref[...] = summed.astype(BF16)
    corner_ref[...] = summed[:8, :BLK]
    mismatch = summed - teacher_ref[...].astype(F32)
    grad = dot(pick, ret_ref[:, D:])
    normed, scale = layer_norm(feats)
    mean_grad = jnp.mean(grad, axis=-1, keepdims=True)
    mean_both = jnp.mean(grad * normed, axis=-1, keepdims=True)
    grad_ref[...] = mismatch + scale * (grad - mean_grad - normed * mean_both)


def total_kernel(mine_in_ref, mine_out_ref, other_in_ref, other_out_ref, after_ref, in_ref, out_ref):
    for q in range(in_ref.shape[0]):
        in_ref[q] = mine_in_ref[q] + other_in_ref[q].astype(F32)
        out_ref[q] = (mine_out_ref[q] + other_out_ref[q].astype(F32)).T


def shift(n_x, dx, dy):
    return [
        (x * 2 + y, ((x + dx) % n_x) * 2 + (y + dy) % 2) for x in range(n_x) for y in range(2)
    ]


VMEM_SPEC = pl.BlockSpec(memory_space=pltpu.VMEM)
SMEM_SPEC = pl.BlockSpec(memory_space=pltpu.SMEM)
HBM_SPEC = pl.BlockSpec(memory_space=pltpu.HBM)


def local(patches, teacher, route, gates, w_in, in_rows, in_cols, w_out, out_rows):
    rows = patches.shape[0]
    owners = lax.axis_size("expert")
    n_x = lax.axis_size("dp") // 2
    slots = owners * SLOT
    share = FB // n_x
    route_row = route.reshape(1, rows)
    gates_row = gates.reshape(1, rows)
    payload = pl.pallas_call(
        pack_kernel,
        out_shape=jax.ShapeDtypeStruct((slots, 2 * D + BLK), BF16),
        in_specs=[VMEM_SPEC] * 2 + [HBM_SPEC] * 2,
        out_specs=HBM_SPEC,
        scratch_shapes=[
            pltpu.VMEM((rows, D), BF16),
            pltpu.VMEM((rows, D), BF16),
            pltpu.VMEM((slots, 2 * D + BLK), BF16),
            pltpu.SemaphoreType.DMA((4,)),
        ],
        compiler_params=pltpu.CompilerParams(vmem_limit_bytes=60 << 20),
        name="pack",
    )(route_row, gates_row, patches, teacher)

    def exchange(values):
        width = values.shape[1]
        blocks = values.reshape(owners, SLOT, width)
        out = lax.all_to_all(blocks, "expert", split_axis=0, concat_axis=0, tiled=True)
        return out.reshape(slots, width)

    arrived = exchange(payload)
    me = lax.axis_index("dp")
    where = jnp.stack([me // 2, me % 2]).astype(jnp.int32)
    part = pltpu.HBM((share, BLK, BLK), BF16)
    returned, *parts = pl.pallas_call(
        expert_kernel,
        out_shape=(pltpu.HBM((slots, 2 * D), BF16),) + (part,) * (2 * n_x),
        in_specs=[SMEM_SPEC] * 4 + [HBM_SPEC, VMEM_SPEC, HBM_SPEC],
        out_specs=(HBM_SPEC,) * (1 + 2 * n_x),
        scratch_shapes=[
            pltpu.VMEM((slots, 2 * D + BLK), BF16),
            pltpu.VMEM((FB, BLK, BLK), BF16),
            pltpu.VMEM((slots, 2 * D), BF16),
            pltpu.VMEM((DB, BLK, slots), BF16),
            pltpu.VMEM((FB, slots, BLK), BF16),
            pltpu.VMEM((FB, slots, BLK), F32),
            pltpu.VMEM((FB, slots, BLK), F32),
            pltpu.VMEM((DB, slots, BLK), F32),
            pltpu.VMEM((2, n_x, share, BLK, BLK), BF16),
            pltpu.VMEM((slots, BLK), F32),
            pltpu.VMEM((DB, slots, BLK), BF16),
            pltpu.VMEM((DB, BLK, slots), BF16),
            pltpu.SemaphoreType.DMA((3,)),
            pltpu.SemaphoreType.DMA((2,)),
            pltpu.SemaphoreType.DMA((2, n_x)),
        ],
        compiler_params=pltpu.CompilerParams(vmem_limit_bytes=51 << 20),
        name="expert",
    )(in_rows[0], in_cols[0], out_rows[0], where, arrived, w_in[0], w_out[0])
    part_in, part_out = parts[:n_x], parts[n_x:]

    back = exchange(returned)
    half = share // 2

    def pass_on(values, dx, dy=0):
        return lax.ppermute(values, "dp", shift(n_x, dx, dy))

    def add(*values):
        return sum(v.astype(F32) for v in values)

    far_in = pass_on(part_in[2], 1)
    far_out = pass_on(part_out[2], 3)
    near_out = pass_on(part_out[1], 1)
    near_in = pass_on(part_in[3], 3)
    pair_in = pass_on(add(part_in[1], far_in).astype(BF16), 1)
    pair_out = pass_on(add(part_out[3], far_out).astype(BF16), 3)
    total_in = add(part_in[0], near_in, pair_in)
    total_out = add(part_out[0], near_out, pair_out)
    other_in = pass_on(total_in[half:].astype(BF16), 0, 1)
    other_out = pass_on(total_out[half:].astype(BF16), 0, 1)
    student, grad_patches, corner = pl.pallas_call(
        finish_kernel,
        out_shape=(
            jax.ShapeDtypeStruct((rows, D), BF16),
            jax.ShapeDtypeStruct((rows, D), F32),
            jax.ShapeDtypeStruct((8, BLK), F32),
        ),
        in_specs=[VMEM_SPEC] * 5,
        out_specs=(VMEM_SPEC,) * 3,
        compiler_params=pltpu.CompilerParams(vmem_limit_bytes=16 << 20),
        name="finish",
    )(route_row, gates_row, patches, teacher, back)
    block = jax.ShapeDtypeStruct((half, BLK, BLK), F32)
    grad_in, grad_out = pl.pallas_call(
        total_kernel,
        out_shape=(block, block),
        in_specs=[VMEM_SPEC] * 5,
        out_specs=(VMEM_SPEC, VMEM_SPEC),
        compiler_params=pltpu.CompilerParams(vmem_limit_bytes=16 << 20),
        name="total",
    )(total_in[:half], total_out[:half], other_in, other_out, corner)
    return (student, grad_patches, grad_in[None], grad_out[None])


def solution(mesh):
    placed = (
        P(("dp", "expert"), None),
        P(("dp", "expert"), None),
        P(("dp", "expert"), None),
        P(("dp", "expert")),
        P("expert", None, None, None),
        P("expert", None),
        P("expert", None),
        P("expert", None, None, None),
        P("expert", None),
    )
    return jax.shard_map(
        local,
        mesh=mesh,
        in_specs=placed,
        out_specs=(
            P(("dp", "expert"), None),
            P(("dp", "expert"), None),
            P("expert", "dp", None, None),
            P("expert", "dp", None, None),
        ),
        check_vma=False,
    )
```

```python
import jax
import jax.numpy as jnp
from jax import lax
from jax.experimental import pallas as pl
from jax.experimental.pallas import tpu as pltpu
from jax.sharding import PartitionSpec as P

BLK = 128
K2 = 4
DB = 10
FB = 40
D = DB * BLK
SLOT = 8
UNROLL = 20
EPS = 1e-06
GELU_K = 0.7978845608028654
GELU_C = 0.044715
F32 = jnp.float32
BF16 = jnp.bfloat16
NT = (((1,), (1,)), ((), ()))


def dot(a, b):
    return jnp.dot(a, b, preferred_element_type=F32)


def dot_nt(a, b):
    return lax.dot_general(a, b, NT, preferred_element_type=F32)


def slot_matrix(route_row, owners):
    rows = route_row.shape[1]
    slots = owners * SLOT
    expert = lax.broadcasted_iota(jnp.int32, (owners, rows), 0)
    hits = expert == route_row
    first = lax.broadcasted_iota(jnp.int32, (rows, rows), 0)
    second = lax.broadcasted_iota(jnp.int32, (rows, rows), 1)
    before = dot(hits.astype(BF16), (first < second).astype(BF16))
    rank = jnp.sum(jnp.where(hits, before, 0.0), axis=0, keepdims=True).astype(jnp.int32)
    slot_row = route_row * SLOT + rank
    slot = lax.broadcasted_iota(jnp.int32, (slots, rows), 0)
    return slot == slot_row


def layer_norm(feats):
    centred = feats - jnp.mean(feats, axis=-1, keepdims=True)
    variance = jnp.mean(centred * centred, axis=-1, keepdims=True)
    scale = lax.rsqrt(variance + EPS)
    return centred * scale, scale


def pack_kernel(route_ref, gates_ref, patches_ref, teacher_ref, out_hbm, out, sems):
    def store(second):
        lanes = pl.ds(second * D, D + second * BLK)
        return pltpu.make_async_copy(out.at[:, lanes], out_hbm.at[:, lanes], sems.at[second])

    owners = out.shape[0] // SLOT
    place = slot_matrix(route_ref[...], owners)
    one_hot = place.astype(BF16)
    feats = patches_ref[...].astype(F32)
    normed, _ = layer_norm(feats)
    out[:, :D] = dot(one_hot, normed.astype(BF16)).astype(BF16)
    early = store(0)
    early.start()
    gates = gates_ref[...].astype(F32)
    gate = jnp.sum(jnp.where(place, gates, 0.0), axis=1, keepdims=True)
    out[:, 2 * D :] = jnp.broadcast_to(gate, (place.shape[0], BLK)).astype(BF16)
    differ = (feats - teacher_ref[...].astype(F32)).astype(BF16)
    out[:, D : 2 * D] = (gate * dot(one_hot, differ)).astype(BF16)
    late = store(1)
    late.start()
    early.wait()
    late.wait()


def expert_kernel(
    in_rows,
    in_cols,
    out_rows,
    where_ref,
    pay_hbm,
    w_in_ref,
    w_out_hbm,
    ret_hbm,
    *rest,
):
    n_x = (len(rest) - 15) // 2
    parts = (rest[:n_x], rest[n_x : 2 * n_x])
    pay_ref, w_out_ref, ret, xnt, hid, slope, gh, gn, grads, gate, ge, get, load_sem, ret_sems, sems = rest[2 * n_x :]
    share = FB // n_x
    half = share // 2
    my_x, my_y = where_ref[0], where_ref[1]
    first, rest_of = pl.ds(0, D), pl.ds(D, D + BLK)
    loads = [
        pltpu.make_async_copy(pay_hbm.at[:, first], pay_ref.at[:, first], load_sem.at[0]),
        pltpu.make_async_copy(pay_hbm.at[:, rest_of], pay_ref.at[:, rest_of], load_sem.at[1]),
        pltpu.make_async_copy(w_out_hbm, w_out_ref, load_sem.at[2]),
    ]
    for load in loads:
        load.start()

    def place(block):
        x = block // share
        y = (block % share) // half
        return lax.rem(x - my_x + n_x, n_x), lax.rem(y - my_y + 2, 2) * half + block % half

    copies = []

    def send(source, target, sem):
        copy = pltpu.make_async_copy(source, target, sem)
        copy.start()
        copies.append(copy)

    def send_rows(kind):
        lanes = pl.ds((1 - kind) * D, D)
        send(ret.at[:, lanes], ret_hbm.at[:, lanes], ret_sems.at[kind])

    def send_part(kind, x):
        send(grads.at[kind, x], parts[kind][x], sems.at[kind, x])

    gn[...] = jnp.zeros_like(gn)
    loads[0].wait()
    for i in range(DB):
        xnt[i] = pay_ref[:, i * BLK : (i + 1) * BLK].T

    def forward(step, carry):
        for q in range(UNROLL):
            b = step * UNROLL + q
            c = in_cols[b]
            lanes = pl.ds(pl.multiple_of(in_rows[b] * BLK, BLK), BLK)
            v = dot(pay_ref[:, lanes], w_in_ref[b])
            v2 = v * v
            t = jnp.tanh(v * (GELU_K + (GELU_K * GELU_C) * v2))
            half_p = 0.5 + 0.5 * t
            active = v * half_p
            hid[c] = active.astype(BF16)
            slope[c] = half_p + (active - active * half_p) * (
                2.0 * GELU_K + (6.0 * GELU_K * GELU_C) * v2
            )
            gh[c] = jnp.zeros_like(v)
        return carry

    lax.fori_loop(0, FB // UNROLL, forward, 0)
    loads[1].wait()
    loads[2].wait()
    gate[...] = jnp.square(pay_ref[:, 2 * D :].astype(F32))

    def read(j):
        return [out_rows[K2 * j + k] for k in range(K2)]

    def spread(j):
        return jnp.concatenate([hid[r] for r in read(j)], axis=1)

    def weight(j):
        return w_out_ref[K2 * j : K2 * (j + 1)].reshape(K2 * BLK, BLK)

    for j in range(DB):
        produced = dot(spread(j), weight(j)).astype(BF16)
        ret[:, j * BLK : (j + 1) * BLK] = produced
        given = pay_ref[:, D + j * BLK : D + (j + 1) * BLK].astype(F32)
        grad = (given + gate[...] * produced.astype(F32)).astype(BF16)
        ge[j] = grad
        get[j] = grad.T
    for j in range(DB):
        outer = dot(get[j], spread(j))
        back = dot_nt(ge[j], weight(j))
        for k, r in enumerate(read(j)):
            rel_x, pos = place(K2 * j + k)
            grads[1, rel_x, pos] = outer[:, k * BLK : (k + 1) * BLK].astype(BF16)
            gh[r] += back[:, k * BLK : (k + 1) * BLK]

    send_rows(1)
    for x in range(n_x):
        send_part(1, x)

    for rel_x in (2, 1, 3, 0):
        x = lax.rem(my_x + rel_x, n_x)
        for q in range(share):
            b = x * share + q
            c = in_cols[b]
            i = in_rows[b]
            grad_pre = (gh[c] * slope[c]).astype(BF16)
            rel_y = q // half
            rel_y = lax.rem(rel_y + my_y, 2)
            grads[0, rel_x, rel_y * half + q % half] = dot(xnt[i], grad_pre).astype(BF16)
            gn[i] += dot_nt(grad_pre, w_in_ref[b])
        send_part(0, rel_x)
    for i in range(DB):
        ret[:, D + i * BLK : D + (i + 1) * BLK] = gn[i].astype(BF16)
    send_rows(0)
    for copy in copies:
        copy.wait()


def finish_kernel(route_ref, gates_ref, patches_ref, teacher_ref, ret_ref, student_ref, grad_ref, corner_ref):
    owners = ret_ref.shape[0] // SLOT
    place = slot_matrix(route_ref[...], owners).astype(F32)
    pick = place.T
    gates = gates_ref[...].astype(F32)
    gated = jnp.broadcast_to(gates, place.shape) * place
    gate = jnp.sum(gated.T, axis=1, keepdims=True)
    pick = pick.astype(BF16)
    feats = patches_ref[...].astype(F32)
    summed = feats + gate * dot(pick, ret_ref[:, :D])
    student_ref[...] = summed.astype(BF16)
    corner_ref[...] = summed[:8, :BLK]
    mismatch = summed - teacher_ref[...].astype(F32)
    grad = dot(pick, ret_ref[:, D:])
    normed, scale = layer_norm(feats)
    mean_grad = jnp.mean(grad, axis=-1, keepdims=True)
    mean_both = jnp.mean(grad * normed, axis=-1, keepdims=True)
    grad_ref[...] = mismatch + scale * (grad - mean_grad - normed * mean_both)


def total_kernel(mine_in_ref, mine_out_ref, other_in_ref, other_out_ref, after_ref, in_ref, out_ref):
    for q in range(in_ref.shape[0]):
        in_ref[q] = mine_in_ref[q] + other_in_ref[q].astype(F32)
        out_ref[q] = (mine_out_ref[q] + other_out_ref[q].astype(F32)).T


def shift(n_x, dx, dy):
    return [
        (x * 2 + y, ((x + dx) % n_x) * 2 + (y + dy) % 2) for x in range(n_x) for y in range(2)
    ]


VMEM_SPEC = pl.BlockSpec(memory_space=pltpu.VMEM)
SMEM_SPEC = pl.BlockSpec(memory_space=pltpu.SMEM)
HBM_SPEC = pl.BlockSpec(memory_space=pltpu.HBM)


def local(patches, teacher, route, gates, w_in, in_rows, in_cols, w_out, out_rows):
    rows = patches.shape[0]
    owners = lax.axis_size("expert")
    n_x = lax.axis_size("dp") // 2
    slots = owners * SLOT
    share = FB // n_x
    route_row = route.reshape(1, rows)
    gates_row = gates.reshape(1, rows)
    payload = pl.pallas_call(
        pack_kernel,
        out_shape=jax.ShapeDtypeStruct((slots, 2 * D + BLK), BF16),
        in_specs=[VMEM_SPEC] * 4,
        out_specs=HBM_SPEC,
        scratch_shapes=[
            pltpu.VMEM((slots, 2 * D + BLK), BF16),
            pltpu.SemaphoreType.DMA((2,)),
        ],
        compiler_params=pltpu.CompilerParams(vmem_limit_bytes=60 << 20),
        name="pack",
    )(route_row, gates_row, patches, teacher)

    def exchange(values):
        width = values.shape[1]
        blocks = values.reshape(owners, SLOT, width)
        out = lax.all_to_all(blocks, "expert", split_axis=0, concat_axis=0, tiled=True)
        return out.reshape(slots, width)

    arrived = exchange(payload)
    me = lax.axis_index("dp")
    where = jnp.stack([me // 2, me % 2]).astype(jnp.int32)
    part = pltpu.HBM((share, BLK, BLK), BF16)
    returned, *parts = pl.pallas_call(
        expert_kernel,
        out_shape=(pltpu.HBM((slots, 2 * D), BF16),) + (part,) * (2 * n_x),
        in_specs=[SMEM_SPEC] * 4 + [HBM_SPEC, VMEM_SPEC, HBM_SPEC],
        out_specs=(HBM_SPEC,) * (1 + 2 * n_x),
        scratch_shapes=[
            pltpu.VMEM((slots, 2 * D + BLK), BF16),
            pltpu.VMEM((FB, BLK, BLK), BF16),
            pltpu.VMEM((slots, 2 * D), BF16),
            pltpu.VMEM((DB, BLK, slots), BF16),
            pltpu.VMEM((FB, slots, BLK), BF16),
            pltpu.VMEM((FB, slots, BLK), F32),
            pltpu.VMEM((FB, slots, BLK), F32),
            pltpu.VMEM((DB, slots, BLK), F32),
            pltpu.VMEM((2, n_x, share, BLK, BLK), BF16),
            pltpu.VMEM((slots, BLK), F32),
            pltpu.VMEM((DB, slots, BLK), BF16),
            pltpu.VMEM((DB, BLK, slots), BF16),
            pltpu.SemaphoreType.DMA((3,)),
            pltpu.SemaphoreType.DMA((2,)),
            pltpu.SemaphoreType.DMA((2, n_x)),
        ],
        compiler_params=pltpu.CompilerParams(vmem_limit_bytes=51 << 20),
        name="expert",
    )(in_rows[0], in_cols[0], out_rows[0], where, arrived, w_in[0], w_out[0])
    part_in, part_out = parts[:n_x], parts[n_x:]

    back = exchange(returned)
    half = share // 2

    def pass_on(values, dx, dy=0):
        return lax.ppermute(values, "dp", shift(n_x, dx, dy))

    def add(*values):
        return sum(v.astype(F32) for v in values)

    far_in = pass_on(part_in[2], 1)
    far_out = pass_on(part_out[2], 3)
    near_out = pass_on(part_out[1], 1)
    near_in = pass_on(part_in[3], 3)
    pair_in = pass_on(add(part_in[1], far_in).astype(BF16), 1)
    pair_out = pass_on(add(part_out[3], far_out).astype(BF16), 3)
    pair_in, near_out = lax.optimization_barrier((pair_in, near_out))
    total_in = add(part_in[0], near_in, pair_in)
    total_out = add(part_out[0], near_out, pair_out)
    other_in = pass_on(total_in[half:].astype(BF16), 0, 1)
    other_out = pass_on(total_out[half:].astype(BF16), 0, 1)
    student, grad_patches, corner = pl.pallas_call(
        finish_kernel,
        out_shape=(
            jax.ShapeDtypeStruct((rows, D), BF16),
            jax.ShapeDtypeStruct((rows, D), F32),
            jax.ShapeDtypeStruct((8, BLK), F32),
        ),
        in_specs=[VMEM_SPEC] * 5,
        out_specs=(VMEM_SPEC,) * 3,
        compiler_params=pltpu.CompilerParams(vmem_limit_bytes=16 << 20),
        name="finish",
    )(route_row, gates_row, patches, teacher, back)
    block = jax.ShapeDtypeStruct((half, BLK, BLK), F32)
    grad_in, grad_out = pl.pallas_call(
        total_kernel,
        out_shape=(block, block),
        in_specs=[VMEM_SPEC] * 5,
        out_specs=(VMEM_SPEC, VMEM_SPEC),
        compiler_params=pltpu.CompilerParams(vmem_limit_bytes=16 << 20),
        name="total",
    )(total_in[:half], total_out[:half], other_in, other_out, corner)
    return (student, grad_patches, grad_in[None], grad_out[None])


def solution(mesh):
    placed = (
        P(("dp", "expert"), None),
        P(("dp", "expert"), None),
        P(("dp", "expert"), None),
        P(("dp", "expert")),
        P("expert", None, None, None),
        P("expert", None),
        P("expert", None),
        P("expert", None, None, None),
        P("expert", None),
    )
    return jax.shard_map(
        local,
        mesh=mesh,
        in_specs=placed,
        out_specs=(
            P(("dp", "expert"), None),
            P(("dp", "expert"), None),
            P("expert", "dp", None, None),
            P("expert", "dp", None, None),
        ),
        check_vma=False,
    )
```

```python
import jax
import jax.numpy as jnp
from jax import lax
from jax.experimental import pallas as pl
from jax.experimental.pallas import tpu as pltpu
from jax.sharding import PartitionSpec as P

BLK = 128
K2 = 4
DB = 10
FB = 40
D = DB * BLK
SLOT = 8
UNROLL = 20
EPS = 1e-06
GELU_K = 0.7978845608028654
GELU_C = 0.044715
F32 = jnp.float32
BF16 = jnp.bfloat16
NT = (((1,), (1,)), ((), ()))


def dot(a, b):
    return jnp.dot(a, b, preferred_element_type=F32)


def dot_nt(a, b):
    return lax.dot_general(a, b, NT, preferred_element_type=F32)


def slot_matrix(route_row, owners):
    rows = route_row.shape[1]
    slots = owners * SLOT
    expert = lax.broadcasted_iota(jnp.int32, (owners, rows), 0)
    hits = expert == route_row
    first = lax.broadcasted_iota(jnp.int32, (rows, rows), 0)
    second = lax.broadcasted_iota(jnp.int32, (rows, rows), 1)
    before = dot(hits.astype(BF16), (first < second).astype(BF16))
    rank = jnp.sum(jnp.where(hits, before, 0.0), axis=0, keepdims=True).astype(jnp.int32)
    slot_row = route_row * SLOT + rank
    slot = lax.broadcasted_iota(jnp.int32, (slots, rows), 0)
    return slot == slot_row


def layer_norm(feats):
    centred = feats - jnp.mean(feats, axis=-1, keepdims=True)
    variance = jnp.mean(centred * centred, axis=-1, keepdims=True)
    scale = lax.rsqrt(variance + EPS)
    return centred * scale, scale


def pack_kernel(route_ref, gates_ref, patches_ref, teacher_ref, out_hbm, out, sems):
    def store(second):
        lanes = pl.ds(second * D, D + second * BLK)
        return pltpu.make_async_copy(out.at[:, lanes], out_hbm.at[:, lanes], sems.at[second])

    owners = out.shape[0] // SLOT
    place = slot_matrix(route_ref[...], owners)
    one_hot = place.astype(BF16)
    feats = patches_ref[...].astype(F32)
    normed, _ = layer_norm(feats)
    out[:, :D] = dot(one_hot, normed.astype(BF16)).astype(BF16)
    early = store(0)
    early.start()
    gates = gates_ref[...].astype(F32)
    gate = jnp.sum(jnp.where(place, gates, 0.0), axis=1, keepdims=True)
    out[:, 2 * D :] = jnp.broadcast_to(gate, (place.shape[0], BLK)).astype(BF16)
    differ = (feats - teacher_ref[...].astype(F32)).astype(BF16)
    out[:, D : 2 * D] = (gate * dot(one_hot, differ)).astype(BF16)
    late = store(1)
    late.start()
    early.wait()
    late.wait()


def expert_kernel(
    in_rows,
    in_cols,
    out_rows,
    where_ref,
    pay_hbm,
    w_in_ref,
    w_out_hbm,
    ret_hbm,
    *rest,
):
    n_x = (len(rest) - 15) // 2
    parts = (rest[:n_x], rest[n_x : 2 * n_x])
    pay_ref, w_out_ref, ret, xnt, hid, slope, gh, gn, grads, gate, ge, get, load_sem, ret_sems, sems = rest[2 * n_x :]
    share = FB // n_x
    half = share // 2
    my_x, my_y = where_ref[0], where_ref[1]
    first, rest_of = pl.ds(0, D), pl.ds(D, D + BLK)
    loads = [
        pltpu.make_async_copy(pay_hbm.at[:, first], pay_ref.at[:, first], load_sem.at[0]),
        pltpu.make_async_copy(pay_hbm.at[:, rest_of], pay_ref.at[:, rest_of], load_sem.at[1]),
        pltpu.make_async_copy(w_out_hbm, w_out_ref, load_sem.at[2]),
    ]
    for load in loads:
        load.start()

    def place(block):
        x = block // share
        y = (block % share) // half
        return lax.rem(x - my_x + n_x, n_x), lax.rem(y - my_y + 2, 2) * half + block % half

    copies = []

    def send(source, target, sem):
        copy = pltpu.make_async_copy(source, target, sem)
        copy.start()
        copies.append(copy)

    def send_rows(start, width, sem):
        lanes = pl.ds(start, width)
        send(ret.at[:, lanes], ret_hbm.at[:, lanes], ret_sems.at[sem])

    def send_part(kind, x):
        send(grads.at[kind, x], parts[kind][x], sems.at[kind, x])

    gn[...] = jnp.zeros_like(gn)
    loads[0].wait()

    def forward(step, carry):
        for q in range(UNROLL):
            b = step * UNROLL + q
            c = in_cols[b]
            lanes = pl.ds(pl.multiple_of(in_rows[b] * BLK, BLK), BLK)
            v = dot(pay_ref[:, lanes], w_in_ref[b])
            v2 = v * v
            t = jnp.tanh(v * (GELU_K + (GELU_K * GELU_C) * v2))
            half_p = 0.5 + 0.5 * t
            active = v * half_p
            hid[c] = active.astype(BF16)
            slope[c] = half_p + (active - active * half_p) * (
                2.0 * GELU_K + (6.0 * GELU_K * GELU_C) * v2
            )
            gh[c] = jnp.zeros_like(v)
        return carry

    lax.fori_loop(0, FB // UNROLL, forward, 0)
    loads[1].wait()
    loads[2].wait()
    gate[...] = jnp.square(pay_ref[:, 2 * D :].astype(F32))

    def read(j):
        return [out_rows[K2 * j + k] for k in range(K2)]

    def spread(j):
        return jnp.concatenate([hid[r] for r in read(j)], axis=1)

    def weight(j):
        return w_out_ref[K2 * j : K2 * (j + 1)].reshape(K2 * BLK, BLK)

    for j in range(DB):
        xnt[j] = pay_ref[:, j * BLK : (j + 1) * BLK].T
        produced = dot(spread(j), weight(j)).astype(BF16)
        ret[:, j * BLK : (j + 1) * BLK] = produced
        given = pay_ref[:, D + j * BLK : D + (j + 1) * BLK].astype(F32)
        grad = (given + gate[...] * produced.astype(F32)).astype(BF16)
        ge[j] = grad
        get[j] = grad.T
    for j in range(DB):
        outer = dot(get[j], spread(j))
        back = dot_nt(ge[j], weight(j))
        for k, r in enumerate(read(j)):
            rel_x, pos = place(K2 * j + k)
            grads[1, rel_x, pos] = outer[:, k * BLK : (k + 1) * BLK].astype(BF16)
            gh[r] += back[:, k * BLK : (k + 1) * BLK]

    send_rows(0, D, 0)
    for x in range(n_x):
        send_part(1, x)

    for rel_x in (2, 1, 3, 0):
        x = lax.rem(my_x + rel_x, n_x)
        for q in range(share):
            b = x * share + q
            c = in_cols[b]
            i = in_rows[b]
            grad_pre = (gh[c] * slope[c]).astype(BF16)
            rel_y = q // half
            rel_y = lax.rem(rel_y + my_y, 2)
            grads[0, rel_x, rel_y * half + q % half] = dot(xnt[i], grad_pre).astype(BF16)
            gn[i] += dot_nt(grad_pre, w_in_ref[b])
        send_part(0, rel_x)
    for i in range(DB):
        ret[:, D + i * BLK : D + (i + 1) * BLK] = gn[i].astype(BF16)
        if i % 2:
            send_rows(D + (i - 1) * BLK, 2 * BLK, 1 + i // 2)
    for copy in copies:
        copy.wait()


def finish_kernel(route_ref, gates_ref, patches_ref, teacher_ref, ret_ref, student_ref, grad_ref, corner_ref):
    owners = ret_ref.shape[0] // SLOT
    place = slot_matrix(route_ref[...], owners).astype(F32)
    pick = place.T
    gates = gates_ref[...].astype(F32)
    gated = jnp.broadcast_to(gates, place.shape) * place
    gate = jnp.sum(gated.T, axis=1, keepdims=True)
    pick = pick.astype(BF16)
    feats = patches_ref[...].astype(F32)
    summed = feats + gate * dot(pick, ret_ref[:, :D])
    student_ref[...] = summed.astype(BF16)
    corner_ref[...] = summed[:8, :BLK]
    mismatch = summed - teacher_ref[...].astype(F32)
    grad = dot(pick, ret_ref[:, D:])
    normed, scale = layer_norm(feats)
    mean_grad = jnp.mean(grad, axis=-1, keepdims=True)
    mean_both = jnp.mean(grad * normed, axis=-1, keepdims=True)
    grad_ref[...] = mismatch + scale * (grad - mean_grad - normed * mean_both)


def total_out_kernel(mine_ref, other_ref, out_ref):
    for q in range(out_ref.shape[0]):
        out_ref[q] = (mine_ref[q] + other_ref[q].astype(F32)).T


def total_in_kernel(mine_ref, other_ref, after_ref, out_ref):
    out_ref[...] = mine_ref[...] + other_ref[...].astype(F32)


def shift(n_x, dx, dy):
    return [
        (x * 2 + y, ((x + dx) % n_x) * 2 + (y + dy) % 2) for x in range(n_x) for y in range(2)
    ]


VMEM_SPEC = pl.BlockSpec(memory_space=pltpu.VMEM)
SMEM_SPEC = pl.BlockSpec(memory_space=pltpu.SMEM)
HBM_SPEC = pl.BlockSpec(memory_space=pltpu.HBM)


def local(patches, teacher, route, gates, w_in, in_rows, in_cols, w_out, out_rows):
    rows = patches.shape[0]
    owners = lax.axis_size("expert")
    n_x = lax.axis_size("dp") // 2
    slots = owners * SLOT
    share = FB // n_x
    route_row = route.reshape(1, rows)
    gates_row = gates.reshape(1, rows)
    payload = pl.pallas_call(
        pack_kernel,
        out_shape=jax.ShapeDtypeStruct((slots, 2 * D + BLK), BF16),
        in_specs=[VMEM_SPEC] * 4,
        out_specs=HBM_SPEC,
        scratch_shapes=[
            pltpu.VMEM((slots, 2 * D + BLK), BF16),
            pltpu.SemaphoreType.DMA((2,)),
        ],
        compiler_params=pltpu.CompilerParams(vmem_limit_bytes=60 << 20),
        name="pack",
    )(route_row, gates_row, patches, teacher)

    def exchange(values):
        width = values.shape[1]
        blocks = values.reshape(owners, SLOT, width)
        out = lax.all_to_all(blocks, "expert", split_axis=0, concat_axis=0, tiled=True)
        return out.reshape(slots, width)

    arrived = exchange(payload)
    me = lax.axis_index("dp")
    where = jnp.stack([me // 2, me % 2]).astype(jnp.int32)
    part = pltpu.HBM((share, BLK, BLK), BF16)
    returned, *parts = pl.pallas_call(
        expert_kernel,
        out_shape=(pltpu.HBM((slots, 2 * D), BF16),) + (part,) * (2 * n_x),
        in_specs=[SMEM_SPEC] * 4 + [HBM_SPEC, VMEM_SPEC, HBM_SPEC],
        out_specs=(HBM_SPEC,) * (1 + 2 * n_x),
        scratch_shapes=[
            pltpu.VMEM((slots, 2 * D + BLK), BF16),
            pltpu.VMEM((FB, BLK, BLK), BF16),
            pltpu.VMEM((slots, 2 * D), BF16),
            pltpu.VMEM((DB, BLK, slots), BF16),
            pltpu.VMEM((FB, slots, BLK), BF16),
            pltpu.VMEM((FB, slots, BLK), F32),
            pltpu.VMEM((FB, slots, BLK), F32),
            pltpu.VMEM((DB, slots, BLK), F32),
            pltpu.VMEM((2, n_x, share, BLK, BLK), BF16),
            pltpu.VMEM((slots, BLK), F32),
            pltpu.VMEM((DB, slots, BLK), BF16),
            pltpu.VMEM((DB, BLK, slots), BF16),
            pltpu.SemaphoreType.DMA((3,)),
            pltpu.SemaphoreType.DMA((6,)),
            pltpu.SemaphoreType.DMA((2, n_x)),
        ],
        compiler_params=pltpu.CompilerParams(vmem_limit_bytes=51 << 20),
        name="expert",
    )(in_rows[0], in_cols[0], out_rows[0], where, arrived, w_in[0], w_out[0])
    part_in, part_out = parts[:n_x], parts[n_x:]

    back = exchange(returned)
    half = share // 2

    def pass_on(values, dx, dy=0):
        return lax.ppermute(values, "dp", shift(n_x, dx, dy))

    def add(*values):
        return sum(v.astype(F32) for v in values)

    far_out = pass_on(part_out[2], 1)
    far_in = pass_on(part_in[2], 3)
    near_in = pass_on(part_in[1], 1)
    near_out = pass_on(part_out[3], 3)
    pair_out = pass_on(add(part_out[1], far_out).astype(BF16), 1)
    pair_in = pass_on(add(part_in[3], far_in).astype(BF16), 3)
    pair_out, near_in = lax.optimization_barrier((pair_out, near_in))
    total_out = add(part_out[0], near_out, pair_out)
    total_in = add(part_in[0], near_in, pair_in)
    other_out = pass_on(total_out[half:].astype(BF16), 0, 1)
    other_in = pass_on(total_in[half:].astype(BF16), 0, 1)
    student, grad_patches, corner = pl.pallas_call(
        finish_kernel,
        out_shape=(
            jax.ShapeDtypeStruct((rows, D), BF16),
            jax.ShapeDtypeStruct((rows, D), F32),
            jax.ShapeDtypeStruct((8, BLK), F32),
        ),
        in_specs=[VMEM_SPEC] * 5,
        out_specs=(VMEM_SPEC,) * 3,
        compiler_params=pltpu.CompilerParams(vmem_limit_bytes=16 << 20),
        name="finish",
    )(route_row, gates_row, patches, teacher, back)
    def total(kernel, *operands):
        return pl.pallas_call(
            kernel,
            out_shape=jax.ShapeDtypeStruct((half, BLK, BLK), F32),
            in_specs=[VMEM_SPEC] * len(operands),
            out_specs=VMEM_SPEC,
            compiler_params=pltpu.CompilerParams(vmem_limit_bytes=16 << 20),
            name="total",
        )(*operands)

    grad_out = total(total_out_kernel, total_out[:half], other_out)
    grad_in = total(total_in_kernel, total_in[:half], other_in, corner)
    return (student, grad_patches, grad_in[None], grad_out[None])


def solution(mesh):
    placed = (
        P(("dp", "expert"), None),
        P(("dp", "expert"), None),
        P(("dp", "expert"), None),
        P(("dp", "expert")),
        P("expert", None, None, None),
        P("expert", None),
        P("expert", None),
        P("expert", None, None, None),
        P("expert", None),
    )
    return jax.shard_map(
        local,
        mesh=mesh,
        in_specs=placed,
        out_specs=(
            P(("dp", "expert"), None),
            P(("dp", "expert"), None),
            P("expert", "dp", None, None),
            P("expert", "dp", None, None),
        ),
        check_vma=False,
    )
```

```python
import jax
import jax.numpy as jnp
from jax import lax
from jax.experimental import pallas as pl
from jax.experimental.pallas import tpu as pltpu
from jax.sharding import PartitionSpec as P

BLK = 128
K2 = 4
DB = 10
FB = 40
D = DB * BLK
SLOT = 8
EPS = 1e-06
GELU_K = 0.7978845608028654
GELU_C = 0.044715
F32 = jnp.float32
BF16 = jnp.bfloat16
NT = (((1,), (1,)), ((), ()))


def dot(a, b):
    return jnp.dot(a, b, preferred_element_type=F32)


def dot_nt(a, b):
    return lax.dot_general(a, b, NT, preferred_element_type=F32)


def slot_matrix(route_row, owners):
    rows = route_row.shape[1]
    slots = owners * SLOT
    expert = lax.broadcasted_iota(jnp.int32, (owners, rows), 0)
    hits = expert == route_row
    first = lax.broadcasted_iota(jnp.int32, (rows, rows), 0)
    second = lax.broadcasted_iota(jnp.int32, (rows, rows), 1)
    before = dot(hits.astype(BF16), (first < second).astype(BF16))
    rank = jnp.sum(jnp.where(hits, before, 0.0), axis=0, keepdims=True).astype(jnp.int32)
    slot_row = route_row * SLOT + rank
    slot = lax.broadcasted_iota(jnp.int32, (slots, rows), 0)
    return slot == slot_row


def layer_norm(feats):
    centred = feats - jnp.mean(feats, axis=-1, keepdims=True)
    variance = jnp.mean(centred * centred, axis=-1, keepdims=True)
    scale = lax.rsqrt(variance + EPS)
    return centred * scale, scale


def pack_kernel(route_ref, gates_ref, patches_ref, teacher_ref, out_hbm, out, sems):
    copies = []

    def store(start, width):
        lanes = pl.ds(start, width)
        copy = pltpu.make_async_copy(
            out.at[:, lanes], out_hbm.at[:, lanes], sems.at[len(copies)]
        )
        copy.start()
        copies.append(copy)

    owners = out.shape[0] // SLOT
    place = slot_matrix(route_ref[...], owners)
    one_hot = place.astype(BF16)
    gates = gates_ref[...].astype(F32)
    gate = jnp.sum(jnp.where(place, gates, 0.0), axis=1, keepdims=True)
    out[:, 2 * D :] = jnp.broadcast_to(gate, (place.shape[0], BLK)).astype(BF16)
    store(2 * D, BLK)
    feats = patches_ref[...].astype(F32)
    differ = (feats - teacher_ref[...].astype(F32)).astype(BF16)
    normed, _ = layer_norm(feats)
    normed = normed.astype(BF16)
    wide = 2 * BLK
    for values, scale, base in ((differ, gate, D), (normed, 1.0, 0)):
        for start in range(0, D, wide):
            lanes = slice(base + start, base + start + wide)
            out[:, lanes] = (scale * dot(one_hot, values[:, start : start + wide])).astype(BF16)
            store(base + start, wide)
    for copy in copies:
        copy.wait()


def expert_kernel(
    in_rows,
    in_cols,
    out_rows,
    where_ref,
    pay_hbm,
    w_in_ref,
    w_out_ref,
    ret_hbm,
    *rest,
):
    n_x = (len(rest) - 14) // 2
    parts = (rest[:n_x], rest[n_x : 2 * n_x])
    pay_ref, ret, xnt, hid, slope, gh, gn, grads, gate, ge, get, load_sem, ret_sems, sems = rest[2 * n_x :]
    share = FB // n_x
    half = share // 2
    my_x, my_y = where_ref[0], where_ref[1]
    first, rest_of = pl.ds(0, D), pl.ds(D, D + BLK)
    loads = [
        pltpu.make_async_copy(pay_hbm.at[:, first], pay_ref.at[:, first], load_sem.at[0]),
        pltpu.make_async_copy(pay_hbm.at[:, rest_of], pay_ref.at[:, rest_of], load_sem.at[1]),
    ]
    loads[0].start()

    def place(block):
        x = block // share
        y = (block % share) // half
        return lax.rem(x - my_x + n_x, n_x), lax.rem(y - my_y + 2, 2) * half + block % half

    copies = []

    def send(source, target, sem):
        copy = pltpu.make_async_copy(source, target, sem)
        copy.start()
        copies.append(copy)

    def send_rows(start, width, sem):
        lanes = pl.ds(start, width)
        send(ret.at[:, lanes], ret_hbm.at[:, lanes], ret_sems.at[sem])

    def send_part(kind, x):
        send(grads.at[kind, x], parts[kind][x], sems.at[kind, x])

    gn[...] = jnp.zeros_like(gn)
    loads[0].wait()
    loads[1].start()

    for b in range(FB):
        c = in_cols[b]
        lanes = pl.ds(pl.multiple_of(in_rows[b] * BLK, BLK), BLK)
        v = dot(pay_ref[:, lanes], w_in_ref[b])
        v2 = v * v
        t = jnp.tanh(v * (GELU_K + (GELU_K * GELU_C) * v2))
        half_p = 0.5 + 0.5 * t
        active = v * half_p
        hid[c] = active.astype(BF16)
        slope[c] = half_p + (active - active * half_p) * (
            2.0 * GELU_K + (6.0 * GELU_K * GELU_C) * v2
        )
        gh[c] = jnp.zeros_like(v)

    loads[1].wait()
    gate[...] = jnp.square(pay_ref[:, 2 * D :].astype(F32))

    def read(j):
        return [out_rows[K2 * j + k] for k in range(K2)]

    def spread(j):
        return jnp.concatenate([hid[r] for r in read(j)], axis=1)

    def weight(j):
        return w_out_ref[K2 * j : K2 * (j + 1)].reshape(K2 * BLK, BLK)

    for j in range(DB):
        xnt[j] = pay_ref[:, j * BLK : (j + 1) * BLK].T
        produced = dot(spread(j), weight(j)).astype(BF16)
        ret[:, j * BLK : (j + 1) * BLK] = produced
        given = pay_ref[:, D + j * BLK : D + (j + 1) * BLK].astype(F32)
        grad = (given + gate[...] * produced.astype(F32)).astype(BF16)
        ge[j] = grad
        get[j] = grad.T
    for j in range(DB):
        outer = dot(get[j], spread(j))
        back = dot_nt(ge[j], weight(j))
        for k, r in enumerate(read(j)):
            rel_x, pos = place(K2 * j + k)
            grads[1, rel_x, pos] = outer[:, k * BLK : (k + 1) * BLK].astype(BF16)
            gh[r] += back[:, k * BLK : (k + 1) * BLK]

    send_rows(0, D, 0)
    for x in range(n_x):
        send_part(1, x)

    for rel_x in (2, 1, 3, 0):
        x = lax.rem(my_x + rel_x, n_x)
        for q in range(share):
            b = x * share + q
            c = in_cols[b]
            i = in_rows[b]
            grad_pre = (gh[c] * slope[c]).astype(BF16)
            rel_y = q // half
            rel_y = lax.rem(rel_y + my_y, 2)
            grads[0, rel_x, rel_y * half + q % half] = dot(xnt[i], grad_pre).astype(BF16)
            gn[i] += dot_nt(grad_pre, w_in_ref[b])
        send_part(0, rel_x)
    for i in range(DB):
        ret[:, D + i * BLK : D + (i + 1) * BLK] = gn[i].astype(BF16)
        if i % 2:
            send_rows(D + (i - 1) * BLK, 2 * BLK, 1 + i // 2)
    for copy in copies:
        copy.wait()


def finish_kernel(route_ref, gates_ref, patches_ref, teacher_ref, ret_ref, student_ref, grad_ref, corner_ref):
    owners = ret_ref.shape[0] // SLOT
    place = slot_matrix(route_ref[...], owners).astype(F32)
    pick = place.T
    gates = gates_ref[...].astype(F32)
    gated = jnp.broadcast_to(gates, place.shape) * place
    gate = jnp.sum(gated.T, axis=1, keepdims=True)
    pick = pick.astype(BF16)
    feats = patches_ref[...].astype(F32)
    summed = feats + gate * dot(pick, ret_ref[:, :D])
    student_ref[...] = summed.astype(BF16)
    corner_ref[...] = summed[:8, :BLK]
    mismatch = summed - teacher_ref[...].astype(F32)
    grad = dot(pick, ret_ref[:, D:])
    normed, scale = layer_norm(feats)
    mean_grad = jnp.mean(grad, axis=-1, keepdims=True)
    mean_both = jnp.mean(grad * normed, axis=-1, keepdims=True)
    grad_ref[...] = mismatch + scale * (grad - mean_grad - normed * mean_both)


def total_kernel(mine_in_ref, mine_out_ref, other_in_ref, other_out_ref, after_ref, in_ref, out_ref):
    for q in range(in_ref.shape[0]):
        in_ref[q] = mine_in_ref[q] + other_in_ref[q].astype(F32)
        out_ref[q] = (mine_out_ref[q] + other_out_ref[q].astype(F32)).T


def shift(n_x, dx, dy):
    return [
        (x * 2 + y, ((x + dx) % n_x) * 2 + (y + dy) % 2) for x in range(n_x) for y in range(2)
    ]


VMEM_SPEC = pl.BlockSpec(memory_space=pltpu.VMEM)
SMEM_SPEC = pl.BlockSpec(memory_space=pltpu.SMEM)
HBM_SPEC = pl.BlockSpec(memory_space=pltpu.HBM)


def local(patches, teacher, route, gates, w_in, in_rows, in_cols, w_out, out_rows):
    rows = patches.shape[0]
    owners = lax.axis_size("expert")
    n_x = lax.axis_size("dp") // 2
    slots = owners * SLOT
    share = FB // n_x
    route_row = route.reshape(1, rows)
    gates_row = gates.reshape(1, rows)
    payload = pl.pallas_call(
        pack_kernel,
        out_shape=jax.ShapeDtypeStruct((slots, 2 * D + BLK), BF16),
        in_specs=[VMEM_SPEC] * 4,
        out_specs=HBM_SPEC,
        scratch_shapes=[
            pltpu.VMEM((slots, 2 * D + BLK), BF16),
            pltpu.SemaphoreType.DMA((11,)),
        ],
        compiler_params=pltpu.CompilerParams(vmem_limit_bytes=60 << 20),
        name="pack",
    )(route_row, gates_row, patches, teacher)

    def exchange(values):
        width = values.shape[1]
        blocks = values.reshape(owners, SLOT, width)
        out = lax.all_to_all(blocks, "expert", split_axis=0, concat_axis=0, tiled=True)
        return out.reshape(slots, width)

    arrived = exchange(payload)
    me = lax.axis_index("dp")
    where = jnp.stack([me // 2, me % 2]).astype(jnp.int32)
    part = pltpu.HBM((share, BLK, BLK), BF16)
    returned, *parts = pl.pallas_call(
        expert_kernel,
        out_shape=(pltpu.HBM((slots, 2 * D), BF16),) + (part,) * (2 * n_x),
        in_specs=[SMEM_SPEC] * 4 + [HBM_SPEC, VMEM_SPEC, VMEM_SPEC],
        out_specs=(HBM_SPEC,) * (1 + 2 * n_x),
        scratch_shapes=[
            pltpu.VMEM((slots, 2 * D + BLK), BF16),
            pltpu.VMEM((slots, 2 * D), BF16),
            pltpu.VMEM((DB, BLK, slots), BF16),
            pltpu.VMEM((FB, slots, BLK), BF16),
            pltpu.VMEM((FB, slots, BLK), F32),
            pltpu.VMEM((FB, slots, BLK), F32),
            pltpu.VMEM((DB, slots, BLK), F32),
            pltpu.VMEM((2, n_x, share, BLK, BLK), BF16),
            pltpu.VMEM((slots, BLK), F32),
            pltpu.VMEM((DB, slots, BLK), BF16),
            pltpu.VMEM((DB, BLK, slots), BF16),
            pltpu.SemaphoreType.DMA((2,)),
            pltpu.SemaphoreType.DMA((6,)),
            pltpu.SemaphoreType.DMA((2, n_x)),
        ],
        compiler_params=pltpu.CompilerParams(vmem_limit_bytes=51 << 20),
        name="expert",
    )(in_rows[0], in_cols[0], out_rows[0], where, arrived, w_in[0], w_out[0])
    part_in, part_out = parts[:n_x], parts[n_x:]

    back = exchange(returned)
    half = share // 2

    def pass_on(values, dx, dy=0):
        return lax.ppermute(values, "dp", shift(n_x, dx, dy))

    def add(*values):
        return sum(v.astype(F32) for v in values)

    far_in = pass_on(part_in[2], 1)
    far_out = pass_on(part_out[2], 3)
    near_out = pass_on(part_out[1], 1)
    near_in = pass_on(part_in[3], 3)
    pair_in = pass_on(add(part_in[1], far_in).astype(BF16), 1)
    pair_out = pass_on(add(part_out[3], far_out).astype(BF16), 3)
    pair_in, near_out = lax.optimization_barrier((pair_in, near_out))
    total_in = add(part_in[0], near_in, pair_in)
    total_out = add(part_out[0], near_out, pair_out)
    other_in = pass_on(total_in[half:].astype(BF16), 0, 1)
    other_out = pass_on(total_out[half:].astype(BF16), 0, 1)
    student, grad_patches, corner = pl.pallas_call(
        finish_kernel,
        out_shape=(
            jax.ShapeDtypeStruct((rows, D), BF16),
            jax.ShapeDtypeStruct((rows, D), F32),
            jax.ShapeDtypeStruct((8, BLK), F32),
        ),
        in_specs=[VMEM_SPEC] * 5,
        out_specs=(VMEM_SPEC,) * 3,
        compiler_params=pltpu.CompilerParams(vmem_limit_bytes=16 << 20),
        name="finish",
    )(route_row, gates_row, patches, teacher, back)
    block = jax.ShapeDtypeStruct((half, BLK, BLK), F32)
    grad_in, grad_out = pl.pallas_call(
        total_kernel,
        out_shape=(block, block),
        in_specs=[VMEM_SPEC] * 5,
        out_specs=(VMEM_SPEC, VMEM_SPEC),
        compiler_params=pltpu.CompilerParams(vmem_limit_bytes=16 << 20),
        name="total",
    )(total_in[:half], total_out[:half], other_in, other_out, corner)
    return (student, grad_patches, grad_in[None], grad_out[None])


def solution(mesh):
    placed = (
        P(("dp", "expert"), None),
        P(("dp", "expert"), None),
        P(("dp", "expert"), None),
        P(("dp", "expert")),
        P("expert", None, None, None),
        P("expert", None),
        P("expert", None),
        P("expert", None, None, None),
        P("expert", None),
    )
    return jax.shard_map(
        local,
        mesh=mesh,
        in_specs=placed,
        out_specs=(
            P(("dp", "expert"), None),
            P(("dp", "expert"), None),
            P("expert", "dp", None, None),
            P("expert", "dp", None, None),
        ),
        check_vma=False,
    )
```

```python
import jax
import jax.numpy as jnp
from jax import lax
from jax.experimental import pallas as pl
from jax.experimental.pallas import tpu as pltpu
from jax.sharding import PartitionSpec as P

BLK = 128
K2 = 4
DB = 10
FB = 40
D = DB * BLK
SLOT = 8
EPS = 1e-06
GELU_K = 0.7978845608028654
GELU_C = 0.044715
F32 = jnp.float32
BF16 = jnp.bfloat16
NT = (((1,), (1,)), ((), ()))


def dot(a, b):
    return jnp.dot(a, b, preferred_element_type=F32)


def dot_nt(a, b):
    return lax.dot_general(a, b, NT, preferred_element_type=F32)


def slot_matrix(route_row, owners):
    rows = route_row.shape[1]
    slots = owners * SLOT
    expert = lax.broadcasted_iota(jnp.int32, (owners, rows), 0)
    hits = expert == route_row
    first = lax.broadcasted_iota(jnp.int32, (rows, rows), 0)
    second = lax.broadcasted_iota(jnp.int32, (rows, rows), 1)
    before = dot(hits.astype(BF16), (first < second).astype(BF16))
    rank = jnp.sum(jnp.where(hits, before, 0.0), axis=0, keepdims=True).astype(jnp.int32)
    slot_row = route_row * SLOT + rank
    slot = lax.broadcasted_iota(jnp.int32, (slots, rows), 0)
    return slot == slot_row


def layer_norm(feats):
    centred = feats - jnp.mean(feats, axis=-1, keepdims=True)
    variance = jnp.mean(centred * centred, axis=-1, keepdims=True)
    scale = lax.rsqrt(variance + EPS)
    return centred * scale, scale


def pack_kernel(route_ref, gates_ref, patches_ref, teacher_ref, out_hbm, out, sems):
    copies = []

    def store(start, width):
        lanes = pl.ds(start, width)
        copy = pltpu.make_async_copy(
            out.at[:, lanes], out_hbm.at[:, lanes], sems.at[len(copies)]
        )
        copy.start()
        copies.append(copy)

    owners = out.shape[0] // SLOT
    place = slot_matrix(route_ref[...], owners)
    one_hot = place.astype(BF16)
    gates = gates_ref[...].astype(F32)
    gate = jnp.sum(jnp.where(place, gates, 0.0), axis=1, keepdims=True)
    out[:, 2 * D :] = jnp.broadcast_to(gate, (place.shape[0], BLK)).astype(BF16)
    store(2 * D, BLK)
    feats = patches_ref[...].astype(F32)
    differ = (feats - teacher_ref[...].astype(F32)).astype(BF16)
    normed, _ = layer_norm(feats)
    normed = normed.astype(BF16)
    wide = 2 * BLK
    for values, scale, base in ((differ, gate, D), (normed, 1.0, 0)):
        for start in range(0, D, wide):
            lanes = slice(base + start, base + start + wide)
            out[:, lanes] = (scale * dot(one_hot, values[:, start : start + wide])).astype(BF16)
            store(base + start, wide)
    for copy in copies:
        copy.wait()


def expert_kernel(
    in_rows,
    in_cols,
    out_rows,
    where_ref,
    pay_ref,
    w_in_ref,
    w_out_ref,
    ret_hbm,
    *rest,
):
    n_x = (len(rest) - 12) // 2
    parts = (rest[:n_x], rest[n_x : 2 * n_x])
    ret, xnt, hid, slope, gh, gn, grads, gate, ge, get, ret_sems, sems = rest[2 * n_x :]
    share = FB // n_x
    half = share // 2
    my_x, my_y = where_ref[0], where_ref[1]

    def place(block):
        x = block // share
        y = (block % share) // half
        return lax.rem(x - my_x + n_x, n_x), lax.rem(y - my_y + 2, 2) * half + block % half

    copies = []

    def send(source, target, sem):
        copy = pltpu.make_async_copy(source, target, sem)
        copy.start()
        copies.append(copy)

    def send_rows(start, width, sem):
        lanes = pl.ds(start, width)
        send(ret.at[:, lanes], ret_hbm.at[:, lanes], ret_sems.at[sem])

    def send_part(kind, x):
        send(grads.at[kind, x], parts[kind][x], sems.at[kind, x])

    gn[...] = jnp.zeros_like(gn)

    for b in range(FB):
        c = in_cols[b]
        lanes = pl.ds(pl.multiple_of(in_rows[b] * BLK, BLK), BLK)
        v = dot(pay_ref[:, lanes], w_in_ref[b])
        v2 = v * v
        t = jnp.tanh(v * (GELU_K + (GELU_K * GELU_C) * v2))
        half_p = 0.5 + 0.5 * t
        active = v * half_p
        hid[c] = active.astype(BF16)
        slope[c] = half_p + (active - active * half_p) * (
            2.0 * GELU_K + (6.0 * GELU_K * GELU_C) * v2
        )
        gh[c] = jnp.zeros_like(v)

    gate[...] = jnp.square(pay_ref[:, 2 * D :].astype(F32))

    def read(j):
        return [out_rows[K2 * j + k] for k in range(K2)]

    def spread(j):
        return jnp.concatenate([hid[r] for r in read(j)], axis=1)

    def weight(j):
        return w_out_ref[K2 * j : K2 * (j + 1)].reshape(K2 * BLK, BLK)

    for j in range(DB):
        xnt[j] = pay_ref[:, j * BLK : (j + 1) * BLK].T
        produced = dot(spread(j), weight(j)).astype(BF16)
        ret[:, j * BLK : (j + 1) * BLK] = produced
        given = pay_ref[:, D + j * BLK : D + (j + 1) * BLK].astype(F32)
        grad = (given + gate[...] * produced.astype(F32)).astype(BF16)
        ge[j] = grad
        get[j] = grad.T
    for j in range(DB):
        outer = dot(get[j], spread(j))
        back = dot_nt(ge[j], weight(j))
        for k, r in enumerate(read(j)):
            rel_x, pos = place(K2 * j + k)
            grads[1, rel_x, pos] = outer[:, k * BLK : (k + 1) * BLK].astype(BF16)
            gh[r] += back[:, k * BLK : (k + 1) * BLK]

    send_rows(0, D, 0)
    for x in range(n_x):
        send_part(1, x)

    for rel_x in (2, 1, 3, 0):
        x = lax.rem(my_x + rel_x, n_x)
        for q in range(share):
            b = x * share + q
            c = in_cols[b]
            i = in_rows[b]
            grad_pre = (gh[c] * slope[c]).astype(BF16)
            rel_y = q // half
            rel_y = lax.rem(rel_y + my_y, 2)
            grads[0, rel_x, rel_y * half + q % half] = dot(xnt[i], grad_pre).astype(BF16)
            gn[i] += dot_nt(grad_pre, w_in_ref[b])
        send_part(0, rel_x)
    for i in range(DB):
        ret[:, D + i * BLK : D + (i + 1) * BLK] = gn[i].astype(BF16)
        if i % 2:
            send_rows(D + (i - 1) * BLK, 2 * BLK, 1 + i // 2)
    for copy in copies:
        copy.wait()


def stage_kernel(w_in_ref, w_out_ref, in_ref, out_ref):
    in_ref[...] = w_in_ref[...]
    out_ref[...] = w_out_ref[...]


def finish_kernel(route_ref, gates_ref, patches_ref, teacher_ref, ret_ref, student_ref, grad_ref, corner_ref):
    owners = ret_ref.shape[0] // SLOT
    place = slot_matrix(route_ref[...], owners).astype(F32)
    pick = place.T
    gates = gates_ref[...].astype(F32)
    gated = jnp.broadcast_to(gates, place.shape) * place
    gate = jnp.sum(gated.T, axis=1, keepdims=True)
    pick = pick.astype(BF16)
    feats = patches_ref[...].astype(F32)
    summed = feats + gate * dot(pick, ret_ref[:, :D])
    student_ref[...] = summed.astype(BF16)
    corner_ref[...] = summed[:8, :BLK]
    mismatch = summed - teacher_ref[...].astype(F32)
    grad = dot(pick, ret_ref[:, D:])
    normed, scale = layer_norm(feats)
    mean_grad = jnp.mean(grad, axis=-1, keepdims=True)
    mean_both = jnp.mean(grad * normed, axis=-1, keepdims=True)
    grad_ref[...] = mismatch + scale * (grad - mean_grad - normed * mean_both)


def total_kernel(mine_in_ref, mine_out_ref, other_in_ref, other_out_ref, after_ref, in_ref, out_ref):
    for q in range(in_ref.shape[0]):
        in_ref[q] = mine_in_ref[q] + other_in_ref[q].astype(F32)
        out_ref[q] = (mine_out_ref[q] + other_out_ref[q].astype(F32)).T


def shift(n_x, dx, dy):
    return [
        (x * 2 + y, ((x + dx) % n_x) * 2 + (y + dy) % 2) for x in range(n_x) for y in range(2)
    ]


VMEM_SPEC = pl.BlockSpec(memory_space=pltpu.VMEM)
SMEM_SPEC = pl.BlockSpec(memory_space=pltpu.SMEM)
HBM_SPEC = pl.BlockSpec(memory_space=pltpu.HBM)


def local(patches, teacher, route, gates, w_in, in_rows, in_cols, w_out, out_rows):
    rows = patches.shape[0]
    owners = lax.axis_size("expert")
    n_x = lax.axis_size("dp") // 2
    slots = owners * SLOT
    share = FB // n_x
    route_row = route.reshape(1, rows)
    gates_row = gates.reshape(1, rows)
    payload = pl.pallas_call(
        pack_kernel,
        out_shape=jax.ShapeDtypeStruct((slots, 2 * D + BLK), BF16),
        in_specs=[VMEM_SPEC] * 4,
        out_specs=HBM_SPEC,
        scratch_shapes=[
            pltpu.VMEM((slots, 2 * D + BLK), BF16),
            pltpu.SemaphoreType.DMA((11,)),
        ],
        compiler_params=pltpu.CompilerParams(vmem_limit_bytes=60 << 20),
        name="pack",
    )(route_row, gates_row, patches, teacher)

    def exchange(values):
        width = values.shape[1]
        blocks = values.reshape(owners, SLOT, width)
        out = lax.all_to_all(blocks, "expert", split_axis=0, concat_axis=0, tiled=True)
        return out.reshape(slots, width)

    arrived = exchange(payload)
    blocks = jax.ShapeDtypeStruct((FB, BLK, BLK), BF16)
    staged_in, staged_out = pl.pallas_call(
        stage_kernel,
        out_shape=(blocks, blocks),
        in_specs=[VMEM_SPEC] * 2,
        out_specs=(VMEM_SPEC, VMEM_SPEC),
        compiler_params=pltpu.CompilerParams(vmem_limit_bytes=16 << 20),
        name="stage",
    )(w_in[0], w_out[0])
    me = lax.axis_index("dp")
    where = jnp.stack([me // 2, me % 2]).astype(jnp.int32)
    part = pltpu.HBM((share, BLK, BLK), BF16)
    returned, *parts = pl.pallas_call(
        expert_kernel,
        out_shape=(pltpu.HBM((slots, 2 * D), BF16),) + (part,) * (2 * n_x),
        in_specs=[SMEM_SPEC] * 4 + [VMEM_SPEC] * 3,
        out_specs=(HBM_SPEC,) * (1 + 2 * n_x),
        scratch_shapes=[
            pltpu.VMEM((slots, 2 * D), BF16),
            pltpu.VMEM((DB, BLK, slots), BF16),
            pltpu.VMEM((FB, slots, BLK), BF16),
            pltpu.VMEM((FB, slots, BLK), F32),
            pltpu.VMEM((FB, slots, BLK), F32),
            pltpu.VMEM((DB, slots, BLK), F32),
            pltpu.VMEM((2, n_x, share, BLK, BLK), BF16),
            pltpu.VMEM((slots, BLK), F32),
            pltpu.VMEM((DB, slots, BLK), BF16),
            pltpu.VMEM((DB, BLK, slots), BF16),
            pltpu.SemaphoreType.DMA((6,)),
            pltpu.SemaphoreType.DMA((2, n_x)),
        ],
        compiler_params=pltpu.CompilerParams(vmem_limit_bytes=30 << 20),
        name="expert",
    )(in_rows[0], in_cols[0], out_rows[0], where, arrived, staged_in, staged_out)
    part_in, part_out = parts[:n_x], parts[n_x:]

    back = exchange(returned)
    half = share // 2

    def pass_on(values, dx, dy=0):
        return lax.ppermute(values, "dp", shift(n_x, dx, dy))

    def add(*values):
        return sum(v.astype(F32) for v in values)

    far_in = pass_on(part_in[2], 1)
    far_out = pass_on(part_out[2], 3)
    near_out = pass_on(part_out[1], 1)
    near_in = pass_on(part_in[3], 3)
    pair_in = pass_on(add(part_in[1], far_in).astype(BF16), 1)
    pair_out = pass_on(add(part_out[3], far_out).astype(BF16), 3)
    pair_in, near_out = lax.optimization_barrier((pair_in, near_out))
    total_in = add(part_in[0], near_in, pair_in)
    total_out = add(part_out[0], near_out, pair_out)
    other_in = pass_on(total_in[half:].astype(BF16), 0, 1)
    other_out = pass_on(total_out[half:].astype(BF16), 0, 1)
    student, grad_patches, corner = pl.pallas_call(
        finish_kernel,
        out_shape=(
            jax.ShapeDtypeStruct((rows, D), BF16),
            jax.ShapeDtypeStruct((rows, D), F32),
            jax.ShapeDtypeStruct((8, BLK), F32),
        ),
        in_specs=[VMEM_SPEC] * 5,
        out_specs=(VMEM_SPEC,) * 3,
        compiler_params=pltpu.CompilerParams(vmem_limit_bytes=16 << 20),
        name="finish",
    )(route_row, gates_row, patches, teacher, back)
    block = jax.ShapeDtypeStruct((half, BLK, BLK), F32)
    grad_in, grad_out = pl.pallas_call(
        total_kernel,
        out_shape=(block, block),
        in_specs=[VMEM_SPEC] * 5,
        out_specs=(VMEM_SPEC, VMEM_SPEC),
        compiler_params=pltpu.CompilerParams(vmem_limit_bytes=16 << 20),
        name="total",
    )(total_in[:half], total_out[:half], other_in, other_out, corner)
    return (student, grad_patches, grad_in[None], grad_out[None])


def solution(mesh):
    placed = (
        P(("dp", "expert"), None),
        P(("dp", "expert"), None),
        P(("dp", "expert"), None),
        P(("dp", "expert")),
        P("expert", None, None, None),
        P("expert", None),
        P("expert", None),
        P("expert", None, None, None),
        P("expert", None),
    )
    return jax.shard_map(
        local,
        mesh=mesh,
        in_specs=placed,
        out_specs=(
            P(("dp", "expert"), None),
            P(("dp", "expert"), None),
            P("expert", "dp", None, None),
            P("expert", "dp", None, None),
        ),
        check_vma=False,
    )
```
